512 devices in a mesh: dp: 4 (over y_lo, core), expert: 128 (over x, y_hi, z).
Axes of the slice: x: 4, y: 8 (y_hi: 4, y_lo: 2; y = y_hi * 2 + y_lo), z: 8, core: 2. Of those that a mesh axis runs over, the one named last changes fastest.
Arguments:
- tokens: bfloat16 [512, 256, 640], P(('dp', 'expert')), may hold values from -96 to 96
- slot_keys: bfloat16 [640, 128], replicated, may hold values from -1 to 1
- w_input: bfloat16 [128, 640, 2560], P('expert', None, 'dp'), may hold values from -0.25 to 0.25
- w_output: bfloat16 [128, 2560, 640], P('expert', 'dp'), may hold values from -0.125 to 0.125
- output_grad: bfloat16 [512, 256, 640], P(('dp', 'expert')), may hold values from -6 to 6
Outputs:
- grad_tokens: bfloat16 [512, 256, 640], P(('dp', 'expert'))
- grad_slot_keys: float32 [640, 128], replicated
- grad_w_input: bfloat16 [128, 640, 2560], P('expert', None, 'dp')
- grad_w_output: bfloat16 [128, 2560, 640], P('expert', 'dp')
The draws below stay inside these ranges and needn't reach their ends.
All inputs are finite; a program needn't handle non-finite values.
Results may differ from the reference program's by a relative error of at most 0.025.
Values may be sent and summed in bfloat16 or wider, within the bound.
A program may use at most 64 MiB of HBM per device.

```python
import jax
import jax.numpy as jnp
from jax import lax

D = 640
H = 2560
PATCHES = 256
EXPERTS = 128
IMAGES = 512
N_DP = 4


def draw_slot_keys(key, part):
    key = jax.random.fold_in(key, 11)
    sample = jnp.clip(jax.random.normal(key, (D, EXPERTS), jnp.float32), -6.0, 6.0)
    return (sample * D ** (-0.5)).astype(jnp.bfloat16)


def draw_tokens(key, part):
    key = jax.random.fold_in(key, 13)
    sample = jnp.clip(jax.random.normal(key, (IMAGES, PATCHES, D), jnp.float32), -6.0, 6.0)
    return sample.astype(jnp.bfloat16)


def shard_levels(own_key, extent, cuts, smallest, largest):
    def one(dim, shards_of):
        heights = jax.random.uniform(jax.random.fold_in(jax.random.fold_in(own_key, 6), dim), (shards_of,), jnp.float32, smallest / len(cuts), largest / len(cuts))
        return jnp.repeat(jnp.exp(heights), extent[dim] // shards_of).reshape((-1,) + (1,) * (len(extent) - dim - 1))

    factor_of = one(*cuts[0])
    for cut in cuts[1:]:
        factor_of = factor_of * one(*cut)
    return factor_of


def normal_values(rng, extent, scale, most, shards=(), dtype=jnp.bfloat16):
    values = scale * jax.random.normal(rng, extent, jnp.float32)
    if shards:
        values = values * shard_levels(rng, extent, shards, -0.22, 0.18)
    return jnp.clip(values, -most, most).astype(dtype)


def setup_inputs(seed: int = 0) -> dict:
    splits = jax.random.split(jax.random.key(seed), 6)
    return {
        "tokens": draw_tokens(jax.random.fold_in(splits[5], 71), 0),
        "slot_keys": draw_slot_keys(jax.random.fold_in(splits[5], 71), 0),
        "w_input": normal_values(splits[2], (EXPERTS, D, H), D ** -0.5, 0.25, ((0, 128), (2, 4))),
        "w_output": normal_values(splits[3], (EXPERTS, H, D), H ** -0.5, 0.125, ((0, 128), (1, 4))),
        "output_grad": normal_values(splits[4], (IMAGES, PATCHES, D), 1.0, 6.0, ((0, 512),)),
    }


def gelu_back(pre_act, upstream):
    value, pullback = jax.vjp(jax.nn.gelu, pre_act)
    return pullback(upstream)[0]

def expert_pass(inputs):
    slot_rows, grad_rows, weight_in, weight_out = inputs
    pre_act = jnp.dot(slot_rows, weight_in, preferred_element_type=jnp.float32)
    activated = jax.nn.gelu(pre_act).astype(jnp.bfloat16)
    act_grad = jnp.dot(grad_rows, weight_out.T, preferred_element_type=jnp.float32)
    pre_grad = gelu_back(pre_act, act_grad).astype(jnp.bfloat16)
    grad_out = jnp.dot(activated.T, grad_rows, preferred_element_type=jnp.float32).astype(jnp.bfloat16)
    grad_in = jnp.dot(slot_rows.T, pre_grad, preferred_element_type=jnp.float32).astype(jnp.bfloat16)
    group_width = H // N_DP
    out_sum = jnp.zeros((slot_rows.shape[0], D), jnp.float32)
    in_sum = jnp.zeros((slot_rows.shape[0], D), jnp.float32)
    for group in range(N_DP):
        lower = group * group_width
        upper = lower + group_width
        out_part = jnp.dot(activated[:, lower:upper], weight_out[lower:upper], preferred_element_type=jnp.float32)
        in_part = jnp.dot(pre_grad[:, lower:upper], weight_in[:, lower:upper].T, preferred_element_type=jnp.float32)
        out_sum = out_sum + out_part.astype(jnp.bfloat16).astype(jnp.float32)
        in_sum = in_sum + in_part.astype(jnp.bfloat16).astype(jnp.float32)
    return (out_sum.astype(jnp.bfloat16), in_sum.astype(jnp.bfloat16), grad_in, grad_out)

def reference(tokens, slot_keys, w_input, w_output, output_grad):
    tokens_wide = tokens.astype(jnp.float32)
    keys_wide = slot_keys.astype(jnp.float32)
    grad_wide = output_grad.astype(jnp.float32)
    logits = jnp.einsum('bmd,ds->bms', tokens_wide, keys_wide)
    dispatch = jax.nn.softmax(logits, axis=1)
    combine = jax.nn.softmax(logits, axis=2)
    dispatch_low = dispatch.astype(jnp.bfloat16)
    combine_low = combine.astype(jnp.bfloat16)
    slot_in = jnp.einsum('bms,bmd->bsd', dispatch_low.astype(jnp.float32), tokens_wide).astype(jnp.bfloat16)
    slot_grad = jnp.einsum('bms,bmd->bsd', combine_low.astype(jnp.float32), grad_wide).astype(jnp.bfloat16)
    slot_out, slot_in_grad, grad_w_input, grad_w_output = lax.map(expert_pass, (jnp.transpose(slot_in, (1, 0, 2)), jnp.transpose(slot_grad, (1, 0, 2)), w_input, w_output))
    slot_out = jnp.transpose(slot_out, (1, 0, 2)).astype(jnp.float32)
    slot_in_grad = jnp.transpose(slot_in_grad, (1, 0, 2)).astype(jnp.float32)
    combine_grad = jnp.einsum('bmd,bsd->bms', grad_wide, slot_out)
    dispatch_grad = jnp.einsum('bmd,bsd->bms', tokens_wide, slot_in_grad)
    logit_grad = combine * (combine_grad - lax.optimization_barrier(jnp.sum(combine * combine_grad, axis=2, keepdims=True)))
    logit_grad = logit_grad + dispatch * (dispatch_grad - lax.optimization_barrier(jnp.sum(dispatch * dispatch_grad, axis=1, keepdims=True)))
    logit_grad = logit_grad.astype(jnp.bfloat16).astype(jnp.float32)
    grad_tokens = jnp.einsum('bms,bsd->bmd', dispatch_low.astype(jnp.float32), slot_in_grad)
    grad_tokens = (grad_tokens + jnp.einsum('bms,ds->bmd', logit_grad, keys_wide)).astype(jnp.bfloat16)
    grad_slot_keys = jnp.einsum('bmd,bms->ds', tokens_wide, logit_grad)
    return (grad_tokens, grad_slot_keys, grad_w_input, grad_w_output)
```

```python
import functools

import jax
import jax.numpy as jnp
from jax import lax
from jax.experimental import pallas as pl
from jax.experimental.pallas import tpu as pltpu
from jax.sharding import PartitionSpec as P

MESH = pl.DeviceIdType.MESH
F32 = jnp.float32
BF16 = jnp.bfloat16
NX, NY, NZ = 4, 4, 8
NE = NX * NY * NZ
D = 640
TALL = (((0,), (0,)), ((), ()))
WIDE = (((1,), (1,)), ((), ()))


def dot(a, b, dims=(((1,), (0,)), ((), ()))):
    return lax.dot_general(a, b, dims, preferred_element_type=F32)


def gelu_pair(v):
    c = 0.7978845608028654
    sq = v * v
    t = jnp.tanh(c * (v + 0.044715 * (sq * v)))
    half = 0.5 * (1.0 + t)
    slope = half + 0.5 * v * (1.0 - t * t) * (c * (1.0 + 3.0 * 0.044715 * sq))
    return v * half, slope


def interleaver():
    r = lax.broadcasted_iota(jnp.int32, (256, 256), 0)
    c = lax.broadcasted_iota(jnp.int32, (256, 256), 1)
    return (r == 2 * (c - 128 * (c >= 128).astype(jnp.int32)) + (c >= 128).astype(jnp.int32)).astype(BF16)


def kernel(
    tok_ref, keys_ref, wi_hbm, wo_hbm, og_ref,
    gt_ref, gk_ref, gwi_ref, gwo_ref,
    wi, wo, dispatch, combine, mix,
    src1, dst1, rows, act, pre_grad, part, sib_in, chip_sum, par_in, src2, dst2,
    key_mine, key_sib, key_split, key_got, key_row, key_rows, key_all,
    w_sem, a1_s, a1_r, g_s, g_r, p_s, p_r, c_s, c_r, a2_s, a2_r,
    k_s, k_r,
):
    g = lax.axis_index("dp")
    e = lax.axis_index("expert")
    core, ylo = g % 2, g // 2
    x, y, z = e // (NY * NZ), (e // NZ) % NY, e % NZ
    sib = (g + 1 - 2 * core, e)
    par = ((g + 2) % 4, e)
    diag = ((g + 3 - 2 * core) % 4, e)

    def nth(k):
        dz = (k % 2) * 4 + ((k // 8) % 2) * 2 + (k // 64) % 2
        dy = ((k // 2) % 2) * 2 + (k // 16) % 2
        dx = ((k // 4) % 2) * 2 + (k // 32) % 2
        return ((x + dx) % NX) * (NY * NZ) + ((y + dy) % NY) * NZ + (z + dz) % NZ

    def plane(k):
        dx, dz = k // NZ, k % NZ
        return ((x + dx) % NX), (z + dz) % NZ

    def line(k):
        yy = (2 * y + ylo + k) % 8
        return ((yy % 2) * 2 + core, x * (NY * NZ) + (yy // 2) * NZ + z)

    def copy(src, dst, s, r, dev):
        return pltpu.make_async_remote_copy(
            src_ref=src, dst_ref=dst, send_sem=s, recv_sem=r,
            device_id=dev, device_id_type=MESH,
        )

    load_i = pltpu.make_async_copy(wi_hbm, wi, w_sem.at[0])
    load_o = pltpu.make_async_copy(wo_hbm, wo, w_sem.at[1])
    load_i.start()
    load_o.start()

    barrier = pltpu.get_barrier_semaphore()

    def greet(k, _):
        pl.semaphore_signal(barrier, inc=1, device_id=(g, (e + k) % NE), device_id_type=MESH)
        return 0

    lax.fori_loop(1, NE, greet, 0)
    for dev in (sib, par, diag):
        pl.semaphore_signal(barrier, inc=1, device_id=dev, device_id_type=MESH)
    for k in range(1, NY):
        other = ((g + 2) % 4, x * (NY * NZ) + ((y + k) % NY) * NZ + z)
        pl.semaphore_signal(barrier, inc=1, device_id=other, device_id_type=MESH)

    tok = tok_ref[...]
    logits = dot(tok, keys_ref[...])
    ex = jnp.exp(logits - jnp.max(logits, axis=0, keepdims=True))
    disp = ex / jnp.sum(ex, axis=0, keepdims=True)
    ex = jnp.exp(logits - jnp.max(logits, axis=1, keepdims=True))
    comb = ex / jnp.sum(ex, axis=1, keepdims=True)
    dispatch[...] = disp
    combine[...] = comb
    slot_in = dot(disp.astype(BF16), tok, TALL).astype(BF16)
    slot_grad = dot(comb.astype(BF16), og_ref[...], TALL).astype(BF16)
    mix[...] = interleaver()
    pair = dot(mix[...], jnp.concatenate([slot_in, slot_grad], axis=0)).astype(BF16)
    src1[...] = pair.reshape(NE, 2, D)
    dst1[pl.ds(e, 1)] = src1[pl.ds(e, 1)]

    pl.semaphore_wait(barrier, NE - 1 + 3 + NY - 1)

    def exchange(src, dst, s, r):
        def step(k, _):
            t = nth(k)
            copy(src.at[t], dst.at[e], s, r, (g, t)).start()
            return 0

        lax.fori_loop(1, NE, step, 0)
        return copy(src.at[pl.ds(0, NE - 1)], dst.at[pl.ds(0, NE - 1)], s, r, sib)

    done1 = exchange(src1, dst1, a1_s, a1_r)
    done1.wait_recv()

    both = dot(mix[...], dst1[...].reshape(2 * NE, D), TALL).astype(BF16)
    rows[0, 0] = both[:NE]
    rows[1, 0] = both[NE:]
    to_par = copy(rows.at[:, 0], rows.at[:, 2], g_s.at[1], g_r.at[1], par)
    to_par.start()
    to_sib = copy(rows.at[:, 0], rows.at[:, 1], g_s.at[0], g_r.at[0], sib)
    to_sib.start()
    fwd = copy(rows.at[:, 2], rows.at[:, 3], g_s.at[2], g_r.at[2], sib)

    load_i.wait()
    load_o.wait()

    def expert(r):
        value, slope = gelu_pair(dot(rows[0, r], wi[...]))
        value = value.astype(BF16)
        act[r] = value
        down = (dot(rows[1, r], wo[...], WIDE) * slope).astype(BF16)
        pre_grad[r] = down
        part[0, r] = dot(value, wo[...]).astype(BF16)
        part[1, r] = dot(down, wi[...], WIDE).astype(BF16)

    expert(0)
    to_sib.wait_recv()
    expert(1)
    give1 = copy(part.at[:, 1], sib_in.at[:, 0], p_s.at[0], p_r.at[0], sib)
    give1.start()
    to_par.wait_recv()
    fwd.start()
    expert(2)
    fwd.wait_recv()
    expert(3)
    give3 = copy(part.at[:, 3], sib_in.at[:, 1], p_s.at[1], p_r.at[1], sib)
    give3.start()
    give3.wait_recv()
    chip_sum[...] = (part[:, 2].astype(F32) + sib_in[:, 1].astype(F32)).astype(BF16)
    cross = copy(chip_sum, par_in, c_s, c_r, par)
    cross.start()

    gwo_ref[...] = dot(act[...].reshape(4 * NE, D), rows[1].reshape(4 * NE, D), TALL).astype(BF16)
    gwi_ref[...] = dot(rows[0].reshape(4 * NE, D), pre_grad[...].reshape(4 * NE, D), TALL).astype(BF16)

    give1.wait_recv()
    near = part[:, 0].astype(F32) + sib_in[:, 0].astype(F32)
    cross.wait_recv()
    total = (near + par_in[...].astype(F32)).astype(BF16).reshape(2 * NE, D)
    src2[...] = dot(mix[...], total).astype(BF16).reshape(NE, 2, D)
    dst2[pl.ds(e, 1)] = src2[pl.ds(e, 1)]
    done2 = exchange(src2, dst2, a2_s, a2_r)
    done2.wait_recv()

    both = dot(mix[...], dst2[...].reshape(2 * NE, D), TALL).astype(BF16)
    slot_out, slot_in_grad = both[:NE], both[NE:]
    tok = tok_ref[...]
    cg = dot(og_ref[...], slot_out, WIDE)
    dg = dot(tok, slot_in_grad, WIDE)
    comb = combine[...]
    disp = dispatch[...]
    lg = comb * (cg - jnp.sum(comb * cg, axis=1, keepdims=True))
    lg = lg + disp * (dg - jnp.sum(disp * dg, axis=0, keepdims=True))
    lg = lg.astype(BF16)
    term = dot(lg, tok, TALL)

    half = NE // 2
    key_mine[...] = term.reshape(2, half, D)
    k0 = copy(key_mine.at[1 - core], key_sib, k_s.at[0], k_r.at[0], sib)
    k0.start()
    grad = dot(disp.astype(BF16), slot_in_grad) + dot(lg, keys_ref[...], WIDE)
    gt_ref[...] = grad.astype(BF16)
    k0.wait_recv()
    mine = x * NZ + z
    nxz = NX * NZ
    key_split[...] = (key_mine[core] + key_sib[...]).reshape(nxz, 2, D)

    def plane_copy(src, dst, i, k):
        xx, zz = plane(k)
        return copy(src(xx * NZ + zz), dst, k_s.at[i], k_r.at[i], (g, xx * (NY * NZ) + y * NZ + zz))

    def scatter(k, _):
        plane_copy(lambda t: key_split.at[t], key_got.at[mine], 1, k).start()
        return 0

    lax.fori_loop(1, nxz, scatter, 0)
    key_got[pl.ds(mine, 1)] = key_split[pl.ds(mine, 1)]
    k1 = copy(key_split.at[pl.ds(0, nxz - 1)], key_got.at[pl.ds(0, nxz - 1)], k_s.at[1], k_r.at[1], sib)
    k1.wait_recv()
    row = jnp.sum(key_got[...], axis=0)
    place = 2 * y + ylo
    key_row[...] = row
    key_rows[pl.ds(place, 1)] = row[None]

    for k in range(1, 8):
        copy(key_row, key_rows.at[place], k_s.at[2], k_r.at[2], line(k)).start()
    k2 = copy(key_rows.at[pl.ds(0, 7)], key_rows.at[pl.ds(0, 7)], k_s.at[2], k_r.at[2], sib)
    k2.wait_recv()
    row = jnp.sum(key_rows[...], axis=0)
    k2.wait_send()
    key_row[...] = row
    key_all[pl.ds(core * nxz + mine, 1)] = row[None]

    def spread(k, _):
        plane_copy(lambda t: key_row, key_all.at[core * nxz + mine], 3, k).start()
        return 0

    lax.fori_loop(1, nxz, spread, 0)
    k3 = copy(key_split.at[pl.ds(0, nxz - 1)], key_got.at[pl.ds(0, nxz - 1)], k_s.at[3], k_r.at[3], sib)
    k3.wait_recv()
    own = key_all.at[pl.ds(core * nxz, nxz)]
    k4 = copy(own, own, k_s.at[4], k_r.at[4], sib)
    k4.start()
    k4.wait_recv()
    gk_ref[...] = key_all[...].reshape(NE, D)

    done1.wait_send()
    to_par.wait_send()
    to_sib.wait_send()
    fwd.wait_send()
    give1.wait_send()
    give3.wait_send()
    cross.wait_send()
    done2.wait_send()
    k0.wait_send()
    k1.wait_send()
    k3.wait_send()
    k4.wait_send()


def body(tokens, slot_keys, w_input, w_output, output_grad):
    vm = pl.BlockSpec(memory_space=pltpu.VMEM)
    anywhere = pl.BlockSpec(memory_space=pl.ANY)
    dma = pltpu.SemaphoreType.DMA
    n = NE
    gt, gk, gwi, gwo = pl.pallas_call(
        kernel,
        out_shape=(
            jax.ShapeDtypeStruct((256, D), BF16),
            jax.ShapeDtypeStruct((n, D), F32),
            jax.ShapeDtypeStruct((D, D), BF16),
            jax.ShapeDtypeStruct((D, D), BF16),
        ),
        in_specs=[vm, vm, anywhere, anywhere, vm],
        out_specs=[vm] * 4,
        scratch_shapes=[
            pltpu.VMEM((D, D), BF16),
            pltpu.VMEM((D, D), BF16),
            pltpu.VMEM((256, n), F32),
            pltpu.VMEM((256, n), F32),
            pltpu.VMEM((256, 256), BF16),
            pltpu.VMEM((n, 2, D), BF16),
            pltpu.VMEM((n, 2, D), BF16),
            pltpu.VMEM((2, 4, n, D), BF16),
            pltpu.VMEM((4, n, D), BF16),
            pltpu.VMEM((4, n, D), BF16),
            pltpu.VMEM((2, 4, n, D), BF16),
            pltpu.VMEM((2, 2, n, D), BF16),
            pltpu.VMEM((2, n, D), BF16),
            pltpu.VMEM((2, n, D), BF16),
            pltpu.VMEM((n, 2, D), BF16),
            pltpu.VMEM((n, 2, D), BF16),
            pltpu.VMEM((2, n // 2, D), F32),
            pltpu.VMEM((n // 2, D), F32),
            pltpu.VMEM((NX * NZ, 2, D), F32),
            pltpu.VMEM((NX * NZ, 2, D), F32),
            pltpu.VMEM((2, D), F32),
            pltpu.VMEM((8, 2, D), F32),
            pltpu.VMEM((2 * NX * NZ, 2, D), F32),
            dma((2,)), dma, dma, dma((3,)), dma((3,)), dma((2,)), dma((2,)), dma, dma, dma, dma,
            dma((5,)), dma((5,)),
        ],
        compiler_params=pltpu.CompilerParams(
            collective_id=0, has_side_effects=True, vmem_limit_bytes=40 << 20
        ),
    )(tokens[0], slot_keys, w_input[0], w_output[0], output_grad[0])
    return gt[None], gk.T, gwi[None], gwo[None]


def solution(mesh):
    placed = (
        P(("dp", "expert"), None, None),
        P(),
        P("expert", None, "dp"),
        P("expert", "dp", None),
        P(("dp", "expert"), None, None),
    )
    return jax.shard_map(
        body,
        mesh=mesh,
        in_specs=placed,
        out_specs=(
            P(("dp", "expert"), None, None),
            P(),
            P("expert", None, "dp"),
            P("expert", "dp", None),
        ),
        check_vma=False,
    )
```

```python
import functools

import jax
import jax.numpy as jnp
from jax import lax
from jax.experimental import pallas as pl
from jax.experimental.pallas import tpu as pltpu
from jax.sharding import PartitionSpec as P

MESH = pl.DeviceIdType.MESH
F32 = jnp.float32
BF16 = jnp.bfloat16
NX, NY, NZ = 4, 4, 8
NE = NX * NY * NZ
HALF = NE // 2
D = 640
TALL = (((0,), (0,)), ((), ()))
WIDE = (((1,), (1,)), ((), ()))


def dot(a, b, dims=(((1,), (0,)), ((), ()))):
    return lax.dot_general(a, b, dims, preferred_element_type=F32)


def gelu_pair(v):
    c = 0.7978845608028654
    sq = v * v
    t = jnp.tanh(c * (v + 0.044715 * (sq * v)))
    half = 0.5 * (1.0 + t)
    slope = half + 0.5 * v * (1.0 - t * t) * (c * (1.0 + 3.0 * 0.044715 * sq))
    return v * half, slope


def interleaver():
    r = lax.broadcasted_iota(jnp.int32, (2 * HALF, 2 * HALF), 0)
    c = lax.broadcasted_iota(jnp.int32, (2 * HALF, 2 * HALF), 1)
    p = (c >= HALF).astype(jnp.int32)
    return (r == 2 * (c - HALF * p) + p).astype(BF16)


def kernel(
    tok_hbm, keys_hbm, wi_hbm, wo_hbm, og_hbm,
    gt_hbm, gk_ref, gwi_hbm, gwo_hbm,
    tok_ref, keys_ref, wi, wo, og_ref, gt, gwi, gwo,
    dispatch, combine, mix,
    src1, dst1, rows, act, pre_grad, part, sib_in, chip_sum, par_in, src2, dst2,
    key_mine, key_sib, key_split, key_got, key_row, key_rows, key_low, key_all,
    w_sem, o_sem, a1_s, a1_r, g_s, g_r, p_s, p_r, c_s, c_r, a2_s, a2_r,
    k_s, k_r,
):
    g = lax.axis_index("dp")
    e = lax.axis_index("expert")
    core, ylo = g % 2, g // 2
    x, y, z = e // (NY * NZ), (e // NZ) % NY, e % NZ
    sib = (g + 1 - 2 * core, e)
    par = ((g + 2) % 4, e)
    diag = ((g + 3 - 2 * core) % 4, e)

    def nth(q, k):
        dy = ((k // 2) % 2) * 2 + (k // 16) % 2
        dx = ((k // 4) % 2) * 2 + (k // 32) % 2
        dz = 2 * ((k % 2) * 2 + (k // 8) % 2) + (q + dx + dy) % 2
        return ((x + dx) % NX) * (NY * NZ) + ((y + dy) % NY) * NZ + (z + dz) % NZ

    def plane(k):
        dx, dz = k // NZ, k % NZ
        return ((x + dx) % NX), (z + dz) % NZ

    def line(k):
        yy = (2 * y + ylo + k) % 8
        return ((yy % 2) * 2 + core, x * (NY * NZ) + (yy // 2) * NZ + z)

    def copy(src, dst, s, r, dev):
        return pltpu.make_async_remote_copy(
            src_ref=src, dst_ref=dst, send_sem=s, recv_sem=r,
            device_id=dev, device_id_type=MESH,
        )

    loads = [
        pltpu.make_async_copy(far, near, w_sem.at[i])
        for i, (far, near) in enumerate((
            (tok_hbm, tok_ref), (keys_hbm, keys_ref), (og_hbm, og_ref), (wi_hbm, wi), (wo_hbm, wo)
        ))
    ]
    for load in loads:
        load.start()

    barrier = pltpu.get_barrier_semaphore()

    def greet(k, _):
        pl.semaphore_signal(barrier, inc=1, device_id=(g, (e + k) % NE), device_id_type=MESH)
        return 0

    lax.fori_loop(1, NE, greet, 0)
    for dev in (sib, par, diag):
        pl.semaphore_signal(barrier, inc=1, device_id=dev, device_id_type=MESH)
    for k in range(1, NY):
        other = ((g + 2) % 4, x * (NY * NZ) + ((y + k) % NY) * NZ + z)
        pl.semaphore_signal(barrier, inc=1, device_id=other, device_id_type=MESH)

    mix[...] = interleaver()

    def pairs(top, low):
        return dot(mix[...], jnp.concatenate([top, low], axis=0)).astype(BF16).reshape(HALF, 2, D)

    def apart(both):
        two = dot(mix[...], both.reshape(2 * HALF, D), TALL).astype(BF16)
        return two[:HALF], two[HALF:]

    loads[0].wait()
    loads[1].wait()
    tok = tok_ref[...]
    logits = dot(tok, keys_ref[...])
    ex = jnp.exp(logits - jnp.max(logits, axis=0, keepdims=True))
    disp = ex / jnp.sum(ex, axis=0, keepdims=True)
    ex = jnp.exp(logits - jnp.max(logits, axis=1, keepdims=True))
    comb = ex / jnp.sum(ex, axis=1, keepdims=True)
    dispatch[...] = disp
    combine[...] = comb
    slot_in = dot(disp.astype(BF16), tok, TALL).astype(BF16)
    loads[2].wait()
    slot_grad = dot(comb.astype(BF16), og_ref[...], TALL).astype(BF16)
    src1[0:HALF] = pairs(slot_in[:HALF], slot_grad[:HALF])
    src1[HALF:NE] = pairs(slot_in[HALF:], slot_grad[HALF:])
    own = e // 2
    dst1[0, pl.ds(own, 1)] = src1[pl.ds(e, 1)]

    pl.semaphore_wait(barrier, NE - 1 + 3 + NY - 1)

    def out_half(q):
        def step(k, _):
            t = nth(q, k)
            copy(src1.at[t], dst1.at[q, own], a1_s.at[q], a1_r.at[q], (g, t)).start()
            return 0

        lax.fori_loop(1 - q, HALF, step, 0)
        some = pl.ds(0, HALF - 1 + q)
        return copy(src1.at[some], dst1.at[q, some], a1_s.at[q], a1_r.at[q], sib)

    def back_half(q):
        def step(k, _):
            t = nth(q, k)
            copy(src2.at[q, t // 2], dst2.at[e], a2_s, a2_r, (g, t)).start()
            return 0

        lax.fori_loop(1 - q, HALF, step, 0)

    outs = [out_half(q) for q in range(2)]
    to_par = [copy(rows.at[:, q], rows.at[:, 4 + 2 * q], g_s.at[q], g_r.at[q], par) for q in range(2)]
    fwd = [
        copy(rows.at[:, 4 + 2 * q], rows.at[:, 5 + 2 * q], g_s.at[2 + q], g_r.at[2 + q], sib)
        for q in range(2)
    ]
    to_sib = copy(rows.at[:, pl.ds(0, 2)], rows.at[:, pl.ds(2, 2)], g_s.at[4], g_r.at[4], sib)
    for q in range(2):
        outs[q].wait_recv()
        rows[0, q], rows[1, q] = apart(dst1[q])
        to_par[q].start()
    to_sib.start()
    loads[3].wait()
    loads[4].wait()

    def expert(i):
        at = pl.ds(2 * i, 2)
        value, slope = gelu_pair(dot(rows[0, at].reshape(NE, D), wi[...]))
        value = value.astype(BF16)
        act[i] = value
        down = (dot(rows[1, at].reshape(NE, D), wo[...], WIDE) * slope).astype(BF16)
        pre_grad[i] = down
        part[0, at] = dot(value, wo[...]).astype(BF16).reshape(2, HALF, D)
        part[1, at] = dot(down, wi[...], WIDE).astype(BF16).reshape(2, HALF, D)

    give = [
        copy(part.at[:, 5 + 2 * q], sib_in.at[:, 2 + q], p_s.at[q], p_r.at[q], sib) for q in range(2)
    ]
    give_near = copy(part.at[:, pl.ds(2, 2)], sib_in.at[:, pl.ds(0, 2)], p_s.at[2], p_r.at[2], sib)
    cross = [copy(chip_sum.at[:, q], par_in.at[:, q], c_s.at[q], c_r.at[q], par) for q in range(2)]

    def add_up(q):
        give[q].wait_recv()
        chip_sum[:, q] = (part[:, 4 + 2 * q].astype(F32) + sib_in[:, 2 + q].astype(F32)).astype(BF16)
        cross[q].start()

    expert(0)
    to_par[0].wait_recv()
    fwd[0].start()
    to_sib.wait_recv()
    expert(1)
    give_near.start()
    fwd[0].wait_recv()
    expert(2)
    give[0].start()
    to_par[1].wait_recv()
    fwd[1].start()
    add_up(0)
    fwd[1].wait_recv()
    expert(3)
    give[1].start()
    add_up(1)

    store_o = pltpu.make_async_copy(gwo, gwo_hbm, o_sem.at[0])
    store_i = pltpu.make_async_copy(gwi, gwi_hbm, o_sem.at[1])
    store_t = pltpu.make_async_copy(gt, gt_hbm, o_sem.at[2])
    give_near.wait_recv()
    for q in range(2):
        near = part[:, q].astype(F32) + sib_in[:, q].astype(F32)
        cross[q].wait_recv()
        total = (near + par_in[:, q].astype(F32)).astype(BF16)
        src2[q] = pairs(total[0], total[1])
        if q == 0:
            dst2[pl.ds(e, 1)] = src2[0, pl.ds(own, 1)]
        back_half(q)
    backs = copy(dst2.at[pl.ds(0, NE - 1)], dst2.at[pl.ds(0, NE - 1)], a2_s, a2_r, sib)

    gwo[...] = dot(act[...].reshape(4 * NE, D), rows[1].reshape(4 * NE, D), TALL).astype(BF16)
    store_o.start()
    gwi[...] = dot(rows[0].reshape(4 * NE, D), pre_grad[...].reshape(4 * NE, D), TALL).astype(BF16)
    store_i.start()
    backs.wait_recv()

    low, high = apart(dst2[0:HALF]), apart(dst2[HALF:NE])
    slot_out = jnp.concatenate([low[0], high[0]], axis=0)
    slot_in_grad = jnp.concatenate([low[1], high[1]], axis=0)
    tok = tok_ref[...]
    cg = dot(og_ref[...], slot_out, WIDE)
    dg = dot(tok, slot_in_grad, WIDE)
    comb = combine[...]
    disp = dispatch[...]
    lg = comb * (cg - jnp.sum(comb * cg, axis=1, keepdims=True))
    lg = lg + disp * (dg - jnp.sum(disp * dg, axis=0, keepdims=True))
    lg = lg.astype(BF16)
    term = dot(lg, tok, TALL)

    key_mine[...] = term.reshape(2, HALF, D)
    k0 = copy(key_mine.at[1 - core], key_sib, k_s.at[0], k_r.at[0], sib)
    k0.start()
    grad = dot(disp.astype(BF16), slot_in_grad) + dot(lg, keys_ref[...], WIDE)
    gt[...] = grad.astype(BF16)
    store_t.start()
    k0.wait_recv()
    mine = x * NZ + z
    nxz = NX * NZ
    key_split[...] = (key_mine[core] + key_sib[...]).astype(BF16).reshape(nxz, 2, D)

    def plane_copy(src, dst, i, k):
        xx, zz = plane(k)
        return copy(src(xx * NZ + zz), dst, k_s.at[i], k_r.at[i], (g, xx * (NY * NZ) + y * NZ + zz))

    def scatter(k, _):
        plane_copy(lambda t: key_split.at[t], key_got.at[mine], 1, k).start()
        return 0

    lax.fori_loop(1, nxz, scatter, 0)
    key_got[pl.ds(mine, 1)] = key_split[pl.ds(mine, 1)]
    k1 = copy(key_split.at[pl.ds(0, nxz - 1)], key_got.at[pl.ds(0, nxz - 1)], k_s.at[1], k_r.at[1], sib)
    k1.wait_recv()
    row = jnp.sum(key_got[...].astype(F32), axis=0)
    place = 2 * y + ylo
    key_row[...] = row
    key_rows[pl.ds(place, 1)] = row[None]

    for k in range(1, 8):
        copy(key_row, key_rows.at[place], k_s.at[2], k_r.at[2], line(k)).start()
    k2 = copy(key_rows.at[pl.ds(0, 7)], key_rows.at[pl.ds(0, 7)], k_s.at[2], k_r.at[2], sib)
    k2.wait_recv()
    row = jnp.sum(key_rows[...], axis=0).astype(BF16)
    key_low[...] = row[None]
    key_all[pl.ds(core * nxz + mine, 1)] = row[None]

    def spread(k, _):
        plane_copy(lambda t: key_low.at[0], key_all.at[core * nxz + mine], 3, k).start()
        return 0

    lax.fori_loop(1, nxz, spread, 0)
    k3 = copy(key_split.at[pl.ds(0, nxz - 1)], key_got.at[pl.ds(0, nxz - 1)], k_s.at[3], k_r.at[3], sib)
    k3.wait_recv()
    held = key_all.at[pl.ds(core * nxz, nxz)]
    k4 = copy(held, held, k_s.at[4], k_r.at[4], sib)
    k4.start()
    k4.wait_recv()
    gk_ref[...] = key_all[...].reshape(NE, D)

    for store in (store_o, store_i, store_t):
        store.wait()
    for done in outs + to_par + fwd + [to_sib] + give + [give_near] + cross + [backs, k0, k1, k2, k3, k4]:
        done.wait_send()


def hand_over(gt, gk, gwi, gwo, gt_out, gk_out, gwi_out, gwo_out, sem):
    moves = [
        pltpu.make_async_copy(a, b, sem.at[i])
        for i, (a, b) in enumerate(((gwi, gwi_out), (gwo, gwo_out), (gt, gt_out)))
    ]
    for move in moves:
        move.start()
    gk_out[...] = gk[...].astype(F32).T
    for move in moves:
        move.wait()


def body(tokens, slot_keys, w_input, w_output, output_grad):
    vm = pl.BlockSpec(memory_space=pltpu.VMEM)
    anywhere = pl.BlockSpec(memory_space=pl.ANY)
    dma = pltpu.SemaphoreType.DMA
    n = NE
    gt, gk, gwi, gwo = pl.pallas_call(
        kernel,
        out_shape=(
            jax.ShapeDtypeStruct((256, D), BF16),
            jax.ShapeDtypeStruct((n, D), BF16),
            jax.ShapeDtypeStruct((D, D), BF16),
            jax.ShapeDtypeStruct((D, D), BF16),
        ),
        in_specs=[anywhere] * 5,
        out_specs=[anywhere, vm, anywhere, anywhere],
        scratch_shapes=[
            pltpu.VMEM((256, D), BF16),
            pltpu.VMEM((D, n), BF16),
            pltpu.VMEM((D, D), BF16),
            pltpu.VMEM((D, D), BF16),
            pltpu.VMEM((256, D), BF16),
            pltpu.VMEM((256, D), BF16),
            pltpu.VMEM((D, D), BF16),
            pltpu.VMEM((D, D), BF16),
            pltpu.VMEM((256, n), F32),
            pltpu.VMEM((256, n), F32),
            pltpu.VMEM((n, n), BF16),
            pltpu.VMEM((n, 2, D), BF16),
            pltpu.VMEM((2, HALF, 2, D), BF16),
            pltpu.VMEM((2, 8, HALF, D), BF16),
            pltpu.VMEM((4, n, D), BF16),
            pltpu.VMEM((4, n, D), BF16),
            pltpu.VMEM((2, 8, HALF, D), BF16),
            pltpu.VMEM((2, 4, HALF, D), BF16),
            pltpu.VMEM((2, 2, HALF, D), BF16),
            pltpu.VMEM((2, 2, HALF, D), BF16),
            pltpu.VMEM((2, HALF, 2, D), BF16),
            pltpu.VMEM((n, 2, D), BF16),
            pltpu.VMEM((2, HALF, D), F32),
            pltpu.VMEM((HALF, D), F32),
            pltpu.VMEM((NX * NZ, 2, D), BF16),
            pltpu.VMEM((NX * NZ, 2, D), BF16),
            pltpu.VMEM((2, D), F32),
            pltpu.VMEM((8, 2, D), F32),
            pltpu.VMEM((1, 2, D), BF16),
            pltpu.VMEM((2 * NX * NZ, 2, D), BF16),
            dma((5,)), dma((3,)), dma((2,)), dma((2,)), dma((5,)), dma((5,)), dma((3,)), dma((3,)),
            dma((2,)), dma((2,)), dma, dma,
            dma((5,)), dma((5,)),
        ],
        compiler_params=pltpu.CompilerParams(
            collective_id=0, has_side_effects=True, vmem_limit_bytes=60 << 20
        ),
    )(tokens[0], slot_keys, w_input[0], w_output[0], output_grad[0])
    gt, gk, gwi, gwo = pl.pallas_call(
        hand_over,
        out_shape=(
            jax.ShapeDtypeStruct((256, D), BF16),
            jax.ShapeDtypeStruct((D, n), F32),
            jax.ShapeDtypeStruct((D, D), BF16),
            jax.ShapeDtypeStruct((D, D), BF16),
        ),
        in_specs=[anywhere, vm, anywhere, anywhere],
        out_specs=[anywhere, vm, anywhere, anywhere],
        scratch_shapes=[dma((3,))],
    )(gt, gk, gwi, gwo)
    return gt[None], gk, gwi[None], gwo[None]


def solution(mesh):
    placed = (
        P(("dp", "expert"), None, None),
        P(),
        P("expert", None, "dp"),
        P("expert", "dp", None),
        P(("dp", "expert"), None, None),
    )
    return jax.shard_map(
        body,
        mesh=mesh,
        in_specs=placed,
        out_specs=(
            P(("dp", "expert"), None, None),
            P(),
            P("expert", None, "dp"),
            P("expert", "dp", None),
        ),
        check_vma=False,
    )
```

```python
import functools

import jax
import jax.numpy as jnp
from jax import lax
from jax.experimental import pallas as pl
from jax.experimental.pallas import tpu as pltpu
from jax.sharding import PartitionSpec as P

MESH = pl.DeviceIdType.MESH
F32 = jnp.float32
BF16 = jnp.bfloat16
NX, NY, NZ = 4, 4, 8
NE = NX * NY * NZ
HALF = NE // 2
D = 640
TALL = (((0,), (0,)), ((), ()))
WIDE = (((1,), (1,)), ((), ()))


def dot(a, b, dims=(((1,), (0,)), ((), ()))):
    return lax.dot_general(a, b, dims, preferred_element_type=F32)


def gelu_pair(v):
    c = 0.7978845608028654
    sq = v * v
    t = jnp.tanh(c * (v + 0.044715 * (sq * v)))
    half = 0.5 * (1.0 + t)
    slope = half + 0.5 * v * (1.0 - t * t) * (c * (1.0 + 3.0 * 0.044715 * sq))
    return v * half, slope


def interleaver():
    r = lax.broadcasted_iota(jnp.int32, (2 * HALF, 2 * HALF), 0)
    c = lax.broadcasted_iota(jnp.int32, (2 * HALF, 2 * HALF), 1)
    p = (c >= HALF).astype(jnp.int32)
    return (r == 2 * (c - HALF * p) + p).astype(BF16)


def kernel(
    tok_hbm, keys_hbm, wi_hbm, wo_hbm, og_hbm,
    gt_hbm, gk_ref, gwi_hbm, gwo_hbm,
    tok_ref, keys_ref, wi, wo, og_ref, gt, gwi, gwo, wi_t, wo_t,
    dispatch, combine, mix,
    src1, dst1, rows, act, pre_grad, part, sib_in, chip_sum, par_in, src2, dst2,
    key_mine, key_sib, key_split, key_got, key_row, key_rows, key_low, key_all,
    w_sem, o_sem, a1_s, a1_r, g_s, g_r, p_s, p_r, c_s, c_r, a2_s, a2_r,
    k_s, k_r,
):
    g = lax.axis_index("dp")
    e = lax.axis_index("expert")
    core, ylo = g % 2, g // 2
    x, y, z = e // (NY * NZ), (e // NZ) % NY, e % NZ
    sib = (g + 1 - 2 * core, e)
    par = ((g + 2) % 4, e)

    def nth(q, k):
        dy = ((k // 2) % 2) * 2 + (k // 16) % 2
        dx = ((k // 4) % 2) * 2 + (k // 32) % 2
        dz = 2 * ((k % 2) * 2 + (k // 8) % 2) + (q + dx + dy) % 2
        return ((x + dx) % NX) * (NY * NZ) + ((y + dy) % NY) * NZ + (z + dz) % NZ

    def near_by(k):
        low, zz = (ylo + k // NZ) % 2, (z + k) % NZ
        return low * NZ + zz, (low * 2 + core, x * (NY * NZ) + y * NZ + zz)

    def far_off(k):
        return (g, ((x + k // NY) % NX) * (NY * NZ) + ((y + k) % NY) * NZ + z)

    def copy(src, dst, s, r, dev):
        return pltpu.make_async_remote_copy(
            src_ref=src, dst_ref=dst, send_sem=s, recv_sem=r,
            device_id=dev, device_id_type=MESH,
        )

    loads = [
        pltpu.make_async_copy(far, near, w_sem.at[i])
        for i, (far, near) in enumerate((
            (tok_hbm, tok_ref), (keys_hbm, keys_ref), (og_hbm, og_ref), (wi_hbm, wi), (wo_hbm, wo)
        ))
    ]
    for load in loads:
        load.start()

    barrier = pltpu.get_barrier_semaphore()

    def greet(k, _):
        pl.semaphore_signal(barrier, inc=1, device_id=(g, (e + k) % NE), device_id_type=MESH)
        return 0

    lax.fori_loop(1, NE, greet, 0)
    pl.semaphore_signal(barrier, inc=1, device_id=sib, device_id_type=MESH)
    for k in range(NZ, 2 * NZ):
        pl.semaphore_signal(barrier, inc=1, device_id=near_by(k)[1], device_id_type=MESH)

    mix[...] = interleaver()

    def pairs(top, low):
        return dot(mix[...], jnp.concatenate([top, low], axis=0)).astype(BF16).reshape(HALF, 2, D)

    def apart(both):
        two = dot(mix[...], both.reshape(2 * HALF, D), TALL).astype(BF16)
        return two[:HALF], two[HALF:]

    loads[0].wait()
    loads[1].wait()
    tok = tok_ref[...]
    logits = dot(tok, keys_ref[...])
    ex = jnp.exp(logits - jnp.max(logits, axis=0, keepdims=True))
    disp = ex / jnp.sum(ex, axis=0, keepdims=True)
    ex = jnp.exp(logits - jnp.max(logits, axis=1, keepdims=True))
    comb = ex / jnp.sum(ex, axis=1, keepdims=True)
    dispatch[...] = disp
    combine[...] = comb
    slot_in = dot(disp.astype(BF16), tok, TALL).astype(BF16)
    loads[2].wait()
    slot_grad = dot(comb.astype(BF16), og_ref[...], TALL).astype(BF16)
    src1[0:HALF] = pairs(slot_in[:HALF], slot_grad[:HALF])
    src1[HALF:NE] = pairs(slot_in[HALF:], slot_grad[HALF:])
    own = e // 2
    dst1[0, pl.ds(own, 1)] = src1[pl.ds(e, 1)]

    loads[3].wait()
    loads[4].wait()
    wi_t[...] = wi[...].T
    wo_t[...] = wo[...].T
    pl.semaphore_wait(barrier, NE + NZ)

    def out_half(q):
        def step(k, _):
            t = nth(q, k)
            copy(src1.at[t], dst1.at[q, own], a1_s.at[q], a1_r.at[q], (g, t)).start()
            return 0

        lax.fori_loop(1 - q, HALF, step, 0)
        some = pl.ds(0, HALF - 1 + q)
        return copy(src1.at[some], dst1.at[q, some], a1_s.at[q], a1_r.at[q], sib)

    def back_half(q):
        def step(k, _):
            t = nth(q, k)
            copy(src2.at[q, t // 2], dst2.at[e], a2_s, a2_r, (g, t)).start()
            return 0

        lax.fori_loop(1 - q, HALF, step, 0)

    outs = [out_half(q) for q in range(2)]
    to_par = [copy(rows.at[:, q], rows.at[:, 4 + 2 * q], g_s.at[q], g_r.at[q], par) for q in range(2)]
    fwd = [
        copy(rows.at[:, 4 + 2 * q], rows.at[:, 5 + 2 * q], g_s.at[2 + q], g_r.at[2 + q], sib)
        for q in range(2)
    ]
    to_sib = copy(rows.at[:, pl.ds(0, 2)], rows.at[:, pl.ds(2, 2)], g_s.at[4], g_r.at[4], sib)
    for q in range(2):
        outs[q].wait_recv()
        rows[0, q], rows[1, q] = apart(dst1[q])
        to_par[q].start()
    to_sib.start()

    def expert(i):
        at = pl.ds(2 * i, 2)
        value, slope = gelu_pair(dot(rows[0, at].reshape(NE, D), wi[...]))
        value = value.astype(BF16)
        act[i] = value
        down = (dot(rows[1, at].reshape(NE, D), wo_t[...]) * slope).astype(BF16)
        pre_grad[i] = down
        part[0, at] = dot(value, wo[...]).astype(BF16).reshape(2, HALF, D)
        part[1, at] = dot(down, wi_t[...]).astype(BF16).reshape(2, HALF, D)

    give = [
        copy(part.at[:, 5 + 2 * q], sib_in.at[:, 2 + q], p_s.at[q], p_r.at[q], sib) for q in range(2)
    ]
    give_near = copy(part.at[:, pl.ds(2, 2)], sib_in.at[:, pl.ds(0, 2)], p_s.at[2], p_r.at[2], sib)
    cross = [copy(chip_sum.at[:, q], par_in.at[:, q], c_s.at[q], c_r.at[q], par) for q in range(2)]

    def add_up(q):
        give[q].wait_recv()
        chip_sum[:, q] = (part[:, 4 + 2 * q].astype(F32) + sib_in[:, 2 + q].astype(F32)).astype(BF16)
        cross[q].start()

    expert(0)
    to_par[0].wait_recv()
    fwd[0].start()
    to_sib.wait_recv()
    expert(1)
    give_near.start()
    fwd[0].wait_recv()
    expert(2)
    give[0].start()
    to_par[1].wait_recv()
    fwd[1].start()
    add_up(0)
    fwd[1].wait_recv()
    expert(3)
    give[1].start()
    add_up(1)

    store_o = pltpu.make_async_copy(gwo, gwo_hbm, o_sem.at[0])
    store_i = pltpu.make_async_copy(gwi, gwi_hbm, o_sem.at[1])
    store_t = pltpu.make_async_copy(gt, gt_hbm, o_sem.at[2])
    give_near.wait_recv()
    for q in range(2):
        near = part[:, q].astype(F32) + sib_in[:, q].astype(F32)
        cross[q].wait_recv()
        total = (near + par_in[:, q].astype(F32)).astype(BF16)
        src2[q] = pairs(total[0], total[1])
        if q == 0:
            dst2[pl.ds(e, 1)] = src2[0, pl.ds(own, 1)]
        back_half(q)
    backs = copy(dst2.at[pl.ds(0, NE - 1)], dst2.at[pl.ds(0, NE - 1)], a2_s, a2_r, sib)

    gwo[...] = dot(act[...].reshape(4 * NE, D), rows[1].reshape(4 * NE, D), TALL).astype(BF16)
    store_o.start()
    gwi[...] = dot(rows[0].reshape(4 * NE, D), pre_grad[...].reshape(4 * NE, D), TALL).astype(BF16)
    store_i.start()
    backs.wait_recv()

    low, high = apart(dst2[0:HALF]), apart(dst2[HALF:NE])
    slot_out = jnp.concatenate([low[0], high[0]], axis=0)
    slot_in_grad = jnp.concatenate([low[1], high[1]], axis=0)
    tok = tok_ref[...]
    cg = dot(og_ref[...], slot_out, WIDE)
    dg = dot(tok, slot_in_grad, WIDE)
    comb = combine[...]
    disp = dispatch[...]
    lg = comb * (cg - jnp.sum(comb * cg, axis=1, keepdims=True))
    lg = lg + disp * (dg - jnp.sum(disp * dg, axis=0, keepdims=True))
    lg = lg.astype(BF16)
    term = dot(lg, tok, TALL)

    key_mine[...] = term.reshape(2, HALF, D)
    k0 = copy(key_mine.at[1 - core], key_sib, k_s.at[0], k_r.at[0], sib)
    k0.start()
    grad = dot(disp.astype(BF16), slot_in_grad) + dot(lg, keys_ref[...], WIDE)
    gt[...] = grad.astype(BF16)
    store_t.start()
    k0.wait_recv()
    key_split[...] = (key_mine[core] + key_sib[...]).astype(BF16).reshape(16, 4, D)
    mine = ylo * NZ + z

    def scatter(k, _):
        t, dev = near_by(k)
        copy(key_split.at[t], key_got.at[mine], k_s.at[1], k_r.at[1], dev).start()
        return 0

    lax.fori_loop(1, 16, scatter, 0)
    key_got[pl.ds(mine, 1)] = key_split[pl.ds(mine, 1)]
    k1 = copy(key_split.at[pl.ds(0, 15)], key_got.at[pl.ds(0, 15)], k_s.at[1], k_r.at[1], sib)
    k1.wait_recv()
    row = jnp.sum(key_got[...].astype(F32), axis=0).astype(BF16)
    place = x * NY + y
    key_row[...] = row[None]
    key_rows[pl.ds(place, 1)] = row[None]

    def share(k, _):
        copy(key_row.at[0], key_rows.at[place], k_s.at[2], k_r.at[2], far_off(k)).start()
        return 0

    lax.fori_loop(1, 16, share, 0)
    k2 = copy(key_rows.at[pl.ds(0, 15)], key_rows.at[pl.ds(0, 15)], k_s.at[2], k_r.at[2], sib)
    k2.wait_recv()
    row = jnp.sum(key_rows[...].astype(F32), axis=0).astype(BF16)
    key_low[...] = row[None]
    key_all[pl.ds(core * 16 + mine, 1)] = row[None]

    def spread(k, _):
        copy(key_low.at[0], key_all.at[core * 16 + mine], k_s.at[3], k_r.at[3], near_by(k)[1]).start()
        return 0

    lax.fori_loop(1, 16, spread, 0)
    k3 = copy(key_split.at[pl.ds(0, 15)], key_got.at[pl.ds(0, 15)], k_s.at[3], k_r.at[3], sib)
    k3.wait_recv()
    held = key_all.at[pl.ds(core * 16, 16)]
    k4 = copy(held, held, k_s.at[4], k_r.at[4], sib)
    k4.start()
    k4.wait_recv()
    gk_ref[...] = key_all[...].reshape(NE, D)

    for store in (store_o, store_i, store_t):
        store.wait()
    for done in outs + to_par + fwd + [to_sib] + give + [give_near] + cross + [backs, k0, k1, k2, k3, k4]:
        done.wait_send()


def hand_over(gt, gk, gwi, gwo, gt_out, gk_out, gwi_out, gwo_out, t, k, turned, i, o, load_sem, store_sem):
    def move(n, a, b):
        return pltpu.make_async_copy(a, b, n)

    loads = [
        move(load_sem.at[n], a, b) for n, (a, b) in enumerate(((gk, k), (gt, t), (gwi, i), (gwo, o)))
    ]
    stores = [
        move(store_sem.at[n], a, b)
        for n, (a, b) in enumerate(((turned, gk_out), (t, gt_out), (i, gwi_out), (o, gwo_out)))
    ]
    for load in loads:
        load.start()
    loads[0].wait()
    turned[...] = k[...].astype(F32).T
    stores[0].start()
    for n in range(1, 4):
        loads[n].wait()
        stores[n].start()
    for store in stores:
        store.wait()


def body(tokens, slot_keys, w_input, w_output, output_grad):
    vm = pl.BlockSpec(memory_space=pltpu.VMEM)
    anywhere = pl.BlockSpec(memory_space=pl.ANY)
    dma = pltpu.SemaphoreType.DMA
    n = NE
    gt, gk, gwi, gwo = pl.pallas_call(
        kernel,
        out_shape=(
            jax.ShapeDtypeStruct((256, D), BF16),
            jax.ShapeDtypeStruct((n, D), BF16),
            jax.ShapeDtypeStruct((D, D), BF16),
            jax.ShapeDtypeStruct((D, D), BF16),
        ),
        in_specs=[anywhere] * 5,
        out_specs=[anywhere, vm, anywhere, anywhere],
        scratch_shapes=[
            pltpu.VMEM((256, D), BF16),
            pltpu.VMEM((D, n), BF16),
            pltpu.VMEM((D, D), BF16),
            pltpu.VMEM((D, D), BF16),
            pltpu.VMEM((256, D), BF16),
            pltpu.VMEM((256, D), BF16),
            pltpu.VMEM((D, D), BF16),
            pltpu.VMEM((D, D), BF16),
            pltpu.VMEM((D, D), BF16),
            pltpu.VMEM((D, D), BF16),
            pltpu.VMEM((256, n), F32),
            pltpu.VMEM((256, n), F32),
            pltpu.VMEM((n, n), BF16),
            pltpu.VMEM((n, 2, D), BF16),
            pltpu.VMEM((2, HALF, 2, D), BF16),
            pltpu.VMEM((2, 8, HALF, D), BF16),
            pltpu.VMEM((4, n, D), BF16),
            pltpu.VMEM((4, n, D), BF16),
            pltpu.VMEM((2, 8, HALF, D), BF16),
            pltpu.VMEM((2, 4, HALF, D), BF16),
            pltpu.VMEM((2, 2, HALF, D), BF16),
            pltpu.VMEM((2, 2, HALF, D), BF16),
            pltpu.VMEM((2, HALF, 2, D), BF16),
            pltpu.VMEM((n, 2, D), BF16),
            pltpu.VMEM((2, HALF, D), F32),
            pltpu.VMEM((HALF, D), F32),
            pltpu.VMEM((16, 4, D), BF16),
            pltpu.VMEM((16, 4, D), BF16),
            pltpu.VMEM((1, 4, D), BF16),
            pltpu.VMEM((16, 4, D), BF16),
            pltpu.VMEM((1, 4, D), BF16),
            pltpu.VMEM((32, 4, D), BF16),
            dma((5,)), dma((3,)), dma((2,)), dma((2,)), dma((5,)), dma((5,)), dma((3,)), dma((3,)),
            dma((2,)), dma((2,)), dma, dma,
            dma((5,)), dma((5,)),
        ],
        compiler_params=pltpu.CompilerParams(
            collective_id=0, has_side_effects=True, vmem_limit_bytes=60 << 20
        ),
    )(tokens[0], slot_keys, w_input[0], w_output[0], output_grad[0])
    gt, gk, gwi, gwo = pl.pallas_call(
        hand_over,
        out_shape=(
            jax.ShapeDtypeStruct((256, D), BF16),
            jax.ShapeDtypeStruct((D, n), F32),
            jax.ShapeDtypeStruct((D, D), BF16),
            jax.ShapeDtypeStruct((D, D), BF16),
        ),
        in_specs=[anywhere] * 4,
        out_specs=[anywhere] * 4,
        scratch_shapes=[
            pltpu.VMEM((256, D), BF16),
            pltpu.VMEM((n, D), BF16),
            pltpu.VMEM((D, n), F32),
            pltpu.VMEM((D, D), BF16),
            pltpu.VMEM((D, D), BF16),
            dma((4,)),
            dma((4,)),
        ],
        compiler_params=pltpu.CompilerParams(vmem_limit_bytes=60 << 20),
    )(gt, gk, gwi, gwo)
    return gt[None], gk, gwi[None], gwo[None]


def solution(mesh):
    placed = (
        P(("dp", "expert"), None, None),
        P(),
        P("expert", None, "dp"),
        P("expert", "dp", None),
        P(("dp", "expert"), None, None),
    )
    return jax.shard_map(
        body,
        mesh=mesh,
        in_specs=placed,
        out_specs=(
            P(("dp", "expert"), None, None),
            P(),
            P("expert", None, "dp"),
            P("expert", "dp", None),
        ),
        check_vma=False,
    )
```

```python
import functools

import jax
import jax.numpy as jnp
from jax import lax
from jax.experimental import pallas as pl
from jax.experimental.pallas import tpu as pltpu
from jax.sharding import PartitionSpec as P

MESH = pl.DeviceIdType.MESH
F32 = jnp.float32
BF16 = jnp.bfloat16
NX, NY, NZ = 4, 4, 8
NE = NX * NY * NZ
HALF = NE // 2
D = 640
TALL = (((0,), (0,)), ((), ()))
WIDE = (((1,), (1,)), ((), ()))


def dot(a, b, dims=(((1,), (0,)), ((), ()))):
    return lax.dot_general(a, b, dims, preferred_element_type=F32)


def gelu_pair(v):
    c = 0.7978845608028654
    sq = v * v
    t = jnp.tanh(c * (v + 0.044715 * (sq * v)))
    half = 0.5 * (1.0 + t)
    slope = half + 0.5 * v * (1.0 - t * t) * (c * (1.0 + 3.0 * 0.044715 * sq))
    return v * half, slope


def interleaver():
    r = lax.broadcasted_iota(jnp.int32, (2 * HALF, 2 * HALF), 0)
    c = lax.broadcasted_iota(jnp.int32, (2 * HALF, 2 * HALF), 1)
    p = (c >= HALF).astype(jnp.int32)
    return (r == 2 * (c - HALF * p) + p).astype(BF16)


def kernel(
    tok_hbm, keys_hbm, wi_hbm, wo_hbm, og_hbm,
    gt_hbm, gk_ref, gwi_hbm, gwo_hbm,
    tok_ref, keys_ref, wi, wo, og_ref, gt, gwi, gwo, wi_t, wo_t,
    dispatch, combine, mix,
    src1, dst1, rows, act, pre_grad, part, sib_in, chip_sum, par_in, src2, dst2,
    key_mine, key_sib, key_split, key_got, key_row, key_rows, key_low, key_all,
    w_sem, o_sem, a1_s, a1_r, g_s, g_r, p_s, p_r, c_s, c_r, a2_s, a2_r,
    k_s, k_r,
):
    g = lax.axis_index("dp")
    e = lax.axis_index("expert")
    core, ylo = g % 2, g // 2
    x, y, z = e // (NY * NZ), (e // NZ) % NY, e % NZ
    sib = (g + 1 - 2 * core, e)
    par = ((g + 2) % 4, e)

    def index(xx, yy, zz):
        return (xx % NX) * (NY * NZ) + (yy % NY) * NZ + zz % NZ

    def turns(q, k):
        dy = ((k // 2) % 2) * 2 + (k // 16) % 2
        dx = ((k // 4) % 2) * 2 + (k // 32) % 2
        return dx, dy, 2 * ((k % 2) * 2 + (k // 8) % 2) + (q + dx + dy) % 2

    def lands(dx, dy, dz):
        low = (dy // 2 + (1 - dy % 2) * ylo) % 2
        return low * 2 + core, index(x + dx, y + dy, z + dz)

    def slot_of(xx, yy, zz):
        return (xx % NX) * (NY * NZ // 2) + (yy % NY) * (NZ // 2) + (zz % NZ) // 2

    def near_by(k):
        low, zz = (ylo + k // NZ) % 2, (z + k) % NZ
        return low * NZ + zz, (low * 2 + core, x * (NY * NZ) + y * NZ + zz)

    def far_off(k):
        return (g, ((x + k // NY) % NX) * (NY * NZ) + ((y + k) % NY) * NZ + z)

    def copy(src, dst, s, r, dev):
        return pltpu.make_async_remote_copy(
            src_ref=src, dst_ref=dst, send_sem=s, recv_sem=r,
            device_id=dev, device_id_type=MESH,
        )

    loads = [
        pltpu.make_async_copy(far, near, w_sem.at[i])
        for i, (far, near) in enumerate((
            (tok_hbm, tok_ref), (keys_hbm, keys_ref), (og_hbm, og_ref), (wi_hbm, wi), (wo_hbm, wo)
        ))
    ]
    for load in loads:
        load.start()

    barrier = pltpu.get_barrier_semaphore()

    def hello(dev):
        pl.semaphore_signal(barrier, inc=1, device_id=dev, device_id_type=MESH)

    def greet(k, _):
        hello(lands(k // (NY * NZ), (k // NZ) % NY, k % NZ))
        return 0

    def greet_more(k, _):
        hello((g, index(x + k // NZ, y + 3 - 2 * ylo, z + k % NZ)))
        return 0

    lax.fori_loop(1, NE, greet, 0)
    lax.fori_loop(0, NX * NZ, greet_more, 0)
    for k in range(NX):
        hello((g, index(x + k, y + 2, z)))
    hello(sib)
    for k in range(NZ, 2 * NZ):
        hello(near_by(k)[1])

    mix[...] = interleaver()

    def pairs(top, low):
        return dot(mix[...], jnp.concatenate([top, low], axis=0)).astype(BF16).reshape(HALF, 2, D)

    def apart(both):
        two = dot(mix[...], both.reshape(2 * HALF, D), TALL).astype(BF16)
        return two[:HALF], two[HALF:]

    loads[0].wait()
    loads[1].wait()
    tok = tok_ref[...]
    logits = dot(tok, keys_ref[...])
    ex = jnp.exp(logits - jnp.max(logits, axis=0, keepdims=True))
    disp = ex / jnp.sum(ex, axis=0, keepdims=True)
    ex = jnp.exp(logits - jnp.max(logits, axis=1, keepdims=True))
    comb = ex / jnp.sum(ex, axis=1, keepdims=True)
    dispatch[...] = disp
    combine[...] = comb
    slot_in = dot(disp.astype(BF16), tok, TALL).astype(BF16)
    loads[2].wait()
    slot_grad = dot(comb.astype(BF16), og_ref[...], TALL).astype(BF16)
    src1[0:HALF] = pairs(slot_in[:HALF], slot_grad[:HALF])
    src1[HALF:NE] = pairs(slot_in[HALF:], slot_grad[HALF:])
    own = e // 2
    dst1[0, pl.ds(own, 1)] = src1[pl.ds(e, 1)]

    loads[3].wait()
    loads[4].wait()
    wi_t[...] = wi[...].T
    wo_t[...] = wo[...].T
    pl.semaphore_wait(barrier, NE - 1 + NX * NZ + NX + 1 + NZ)

    def out_half(q):
        def step(k, _):
            dx, dy, dz = turns(q, k)
            dev = lands(dx, dy, dz)
            at = slot_of(x, y + (dy % 2) * (dy + 3 + 2 * ylo), z)
            copy(src1.at[dev[1]], dst1.at[q, at], a1_s.at[q], a1_r.at[q], dev).start()
            return 0

        lax.fori_loop(1 - q, HALF, step, 0)
        some = pl.ds(0, HALF - 1 + q)
        return copy(src1.at[some], dst1.at[q, some], a1_s.at[q], a1_r.at[q], sib)

    def back_half(q):
        def step(k, _):
            dx, dy, dz = turns(q, k)
            odd, upper = dy % 2, dy // 2
            low = (upper + odd + (1 - odd) * ylo) % 2
            yy = y + odd * (3 + 2 * ylo) + (1 - odd) * dy
            at = slot_of(x + dx, y + dy, z + dz)
            dev = (low * 2 + core, index(x + dx, yy, z + dz))
            copy(src2.at[q, at], dst2.at[e], a2_s, a2_r, dev).start()
            return 0

        lax.fori_loop(1 - q, HALF, step, 0)

    outs = [out_half(q) for q in range(2)]
    to_par = [copy(rows.at[:, q], rows.at[:, 4 + 2 * q], g_s.at[q], g_r.at[q], par) for q in range(2)]
    fwd = [
        copy(rows.at[:, 4 + 2 * q], rows.at[:, 5 + 2 * q], g_s.at[2 + q], g_r.at[2 + q], sib)
        for q in range(2)
    ]
    to_sib = copy(rows.at[:, pl.ds(0, 2)], rows.at[:, pl.ds(2, 2)], g_s.at[4], g_r.at[4], sib)
    for q in range(2):
        outs[q].wait_recv()
        rows[0, q], rows[1, q] = apart(dst1[q])
        to_par[q].start()
    to_sib.start()

    def expert(i):
        at = pl.ds(2 * i, 2)
        value, slope = gelu_pair(dot(rows[0, at].reshape(NE, D), wi[...]))
        value = value.astype(BF16)
        act[i] = value
        down = (dot(rows[1, at].reshape(NE, D), wo_t[...]) * slope).astype(BF16)
        pre_grad[i] = down
        part[0, at] = dot(value, wo[...]).astype(BF16).reshape(2, HALF, D)
        part[1, at] = dot(down, wi_t[...]).astype(BF16).reshape(2, HALF, D)

    give = [
        copy(part.at[:, 5 + 2 * q], sib_in.at[:, 2 + q], p_s.at[q], p_r.at[q], sib) for q in range(2)
    ]
    give_near = copy(part.at[:, pl.ds(2, 2)], sib_in.at[:, pl.ds(0, 2)], p_s.at[2], p_r.at[2], sib)
    cross = [copy(chip_sum.at[:, q], par_in.at[:, q], c_s.at[q], c_r.at[q], par) for q in range(2)]

    def add_up(q):
        give[q].wait_recv()
        chip_sum[:, q] = (part[:, 4 + 2 * q].astype(F32) + sib_in[:, 2 + q].astype(F32)).astype(BF16)
        cross[q].start()

    expert(0)
    to_par[0].wait_recv()
    fwd[0].start()
    to_sib.wait_recv()
    expert(1)
    give_near.start()
    fwd[0].wait_recv()
    expert(2)
    give[0].start()
    to_par[1].wait_recv()
    fwd[1].start()
    add_up(0)
    fwd[1].wait_recv()
    expert(3)
    give[1].start()
    add_up(1)

    store_o = pltpu.make_async_copy(gwo, gwo_hbm, o_sem.at[0])
    store_i = pltpu.make_async_copy(gwi, gwi_hbm, o_sem.at[1])
    store_t = pltpu.make_async_copy(gt, gt_hbm, o_sem.at[2])
    give_near.wait_recv()
    for q in range(2):
        near = part[:, q].astype(F32) + sib_in[:, q].astype(F32)
        cross[q].wait_recv()
        total = (near + par_in[:, q].astype(F32)).astype(BF16)
        src2[q] = pairs(total[0], total[1])
        if q == 0:
            dst2[pl.ds(e, 1)] = src2[0, pl.ds(own, 1)]
        back_half(q)
    backs = copy(dst2.at[pl.ds(0, NE - 1)], dst2.at[pl.ds(0, NE - 1)], a2_s, a2_r, sib)

    gwo[...] = dot(act[...].reshape(4 * NE, D), rows[1].reshape(4 * NE, D), TALL).astype(BF16)
    store_o.start()
    gwi[...] = dot(rows[0].reshape(4 * NE, D), pre_grad[...].reshape(4 * NE, D), TALL).astype(BF16)
    store_i.start()
    backs.wait_recv()

    low, high = apart(dst2[0:HALF]), apart(dst2[HALF:NE])
    slot_out = jnp.concatenate([low[0], high[0]], axis=0)
    slot_in_grad = jnp.concatenate([low[1], high[1]], axis=0)
    tok = tok_ref[...]
    cg = dot(og_ref[...], slot_out, WIDE)
    dg = dot(tok, slot_in_grad, WIDE)
    comb = combine[...]
    disp = dispatch[...]
    lg = comb * (cg - jnp.sum(comb * cg, axis=1, keepdims=True))
    lg = lg + disp * (dg - jnp.sum(disp * dg, axis=0, keepdims=True))
    lg = lg.astype(BF16)
    term = dot(lg, tok, TALL)

    key_mine[...] = term.reshape(2, HALF, D)
    k0 = copy(key_mine.at[1 - core], key_sib, k_s.at[0], k_r.at[0], sib)
    k0.start()
    grad = dot(disp.astype(BF16), slot_in_grad) + dot(lg, keys_ref[...], WIDE)
    gt[...] = grad.astype(BF16)
    store_t.start()
    k0.wait_recv()
    key_split[...] = (key_mine[core] + key_sib[...]).astype(BF16).reshape(16, 4, D)
    mine = ylo * NZ + z

    def scatter(k, _):
        t, dev = near_by(k)
        copy(key_split.at[t], key_got.at[mine], k_s.at[1], k_r.at[1], dev).start()
        return 0

    lax.fori_loop(1, 16, scatter, 0)
    key_got[pl.ds(mine, 1)] = key_split[pl.ds(mine, 1)]
    k1 = copy(key_split.at[pl.ds(0, 15)], key_got.at[pl.ds(0, 15)], k_s.at[1], k_r.at[1], sib)
    k1.wait_recv()
    row = jnp.sum(key_got[...].astype(F32), axis=0).astype(BF16)
    place = x * NY + y
    key_row[...] = row[None]
    key_rows[pl.ds(place, 1)] = row[None]

    def share(k, _):
        copy(key_row.at[0], key_rows.at[place], k_s.at[2], k_r.at[2], far_off(k)).start()
        return 0

    lax.fori_loop(1, 16, share, 0)
    k2 = copy(key_rows.at[pl.ds(0, 15)], key_rows.at[pl.ds(0, 15)], k_s.at[2], k_r.at[2], sib)
    k2.wait_recv()
    row = jnp.sum(key_rows[...].astype(F32), axis=0).astype(BF16)
    key_low[...] = row[None]
    key_all[pl.ds(core * 16 + mine, 1)] = row[None]

    def spread(k, _):
        copy(key_low.at[0], key_all.at[core * 16 + mine], k_s.at[3], k_r.at[3], near_by(k)[1]).start()
        return 0

    lax.fori_loop(1, 16, spread, 0)
    k3 = copy(key_split.at[pl.ds(0, 15)], key_got.at[pl.ds(0, 15)], k_s.at[3], k_r.at[3], sib)
    k3.wait_recv()
    held = key_all.at[pl.ds(core * 16, 16)]
    k4 = copy(held, held, k_s.at[4], k_r.at[4], sib)
    k4.start()
    k4.wait_recv()
    gk_ref[...] = key_all[...].reshape(NE, D)

    for store in (store_o, store_i, store_t):
        store.wait()
    for done in outs + to_par + fwd + [to_sib] + give + [give_near] + cross + [backs, k0, k1, k2, k3, k4]:
        done.wait_send()


def hand_over(gt, gk, gwi, gwo, gt_out, gk_out, gwi_out, gwo_out, t, k, turned, i, o, load_sem, store_sem):
    def move(n, a, b):
        return pltpu.make_async_copy(a, b, n)

    loads = [
        move(load_sem.at[n], a, b) for n, (a, b) in enumerate(((gk, k), (gt, t), (gwi, i), (gwo, o)))
    ]
    stores = [
        move(store_sem.at[n], a, b)
        for n, (a, b) in enumerate(((turned, gk_out), (t, gt_out), (i, gwi_out), (o, gwo_out)))
    ]
    for load in loads:
        load.start()
    loads[0].wait()
    turned[...] = k[...].astype(F32).T
    stores[0].start()
    for n in range(1, 4):
        loads[n].wait()
        stores[n].start()
    for store in stores:
        store.wait()


def body(tokens, slot_keys, w_input, w_output, output_grad):
    vm = pl.BlockSpec(memory_space=pltpu.VMEM)
    anywhere = pl.BlockSpec(memory_space=pl.ANY)
    dma = pltpu.SemaphoreType.DMA
    n = NE
    gt, gk, gwi, gwo = pl.pallas_call(
        kernel,
        out_shape=(
            jax.ShapeDtypeStruct((256, D), BF16),
            jax.ShapeDtypeStruct((n, D), BF16),
            jax.ShapeDtypeStruct((D, D), BF16),
            jax.ShapeDtypeStruct((D, D), BF16),
        ),
        in_specs=[anywhere] * 5,
        out_specs=[anywhere, vm, anywhere, anywhere],
        scratch_shapes=[
            pltpu.VMEM((256, D), BF16),
            pltpu.VMEM((D, n), BF16),
            pltpu.VMEM((D, D), BF16),
            pltpu.VMEM((D, D), BF16),
            pltpu.VMEM((256, D), BF16),
            pltpu.VMEM((256, D), BF16),
            pltpu.VMEM((D, D), BF16),
            pltpu.VMEM((D, D), BF16),
            pltpu.VMEM((D, D), BF16),
            pltpu.VMEM((D, D), BF16),
            pltpu.VMEM((256, n), F32),
            pltpu.VMEM((256, n), F32),
            pltpu.VMEM((n, n), BF16),
            pltpu.VMEM((n, 2, D), BF16),
            pltpu.VMEM((2, HALF, 2, D), BF16),
            pltpu.VMEM((2, 8, HALF, D), BF16),
            pltpu.VMEM((4, n, D), BF16),
            pltpu.VMEM((4, n, D), BF16),
            pltpu.VMEM((2, 8, HALF, D), BF16),
            pltpu.VMEM((2, 4, HALF, D), BF16),
            pltpu.VMEM((2, 2, HALF, D), BF16),
            pltpu.VMEM((2, 2, HALF, D), BF16),
            pltpu.VMEM((2, HALF, 2, D), BF16),
            pltpu.VMEM((n, 2, D), BF16),
            pltpu.VMEM((2, HALF, D), F32),
            pltpu.VMEM((HALF, D), F32),
            pltpu.VMEM((16, 4, D), BF16),
            pltpu.VMEM((16, 4, D), BF16),
            pltpu.VMEM((1, 4, D), BF16),
            pltpu.VMEM((16, 4, D), BF16),
            pltpu.VMEM((1, 4, D), BF16),
            pltpu.VMEM((32, 4, D), BF16),
            dma((5,)), dma((3,)), dma((2,)), dma((2,)), dma((5,)), dma((5,)), dma((3,)), dma((3,)),
            dma((2,)), dma((2,)), dma, dma,
            dma((5,)), dma((5,)),
        ],
        compiler_params=pltpu.CompilerParams(
            collective_id=0, has_side_effects=True, vmem_limit_bytes=60 << 20
        ),
    )(tokens[0], slot_keys, w_input[0], w_output[0], output_grad[0])
    gt, gk, gwi, gwo = pl.pallas_call(
        hand_over,
        out_shape=(
            jax.ShapeDtypeStruct((256, D), BF16),
            jax.ShapeDtypeStruct((D, n), F32),
            jax.ShapeDtypeStruct((D, D), BF16),
            jax.ShapeDtypeStruct((D, D), BF16),
        ),
        in_specs=[anywhere] * 4,
        out_specs=[anywhere] * 4,
        scratch_shapes=[
            pltpu.VMEM((256, D), BF16),
            pltpu.VMEM((n, D), BF16),
            pltpu.VMEM((D, n), F32),
            pltpu.VMEM((D, D), BF16),
            pltpu.VMEM((D, D), BF16),
            dma((4,)),
            dma((4,)),
        ],
        compiler_params=pltpu.CompilerParams(vmem_limit_bytes=60 << 20),
    )(gt, gk, gwi, gwo)
    return gt[None], gk, gwi[None], gwo[None]


def solution(mesh):
    placed = (
        P(("dp", "expert"), None, None),
        P(),
        P("expert", None, "dp"),
        P("expert", "dp", None),
        P(("dp", "expert"), None, None),
    )
    return jax.shard_map(
        body,
        mesh=mesh,
        in_specs=placed,
        out_specs=(
            P(("dp", "expert"), None, None),
            P(),
            P("expert", None, "dp"),
            P("expert", "dp", None),
        ),
        check_vma=False,
    )
```

```python
import functools

import jax
import jax.numpy as jnp
from jax import lax
from jax.experimental import pallas as pl
from jax.experimental.pallas import tpu as pltpu
from jax.sharding import PartitionSpec as P

MESH = pl.DeviceIdType.MESH
F32 = jnp.float32
BF16 = jnp.bfloat16
NX, NY, NZ = 4, 4, 8
NE = NX * NY * NZ
HALF = NE // 2
D = 640
TALL = (((0,), (0,)), ((), ()))
WIDE = (((1,), (1,)), ((), ()))


def dot(a, b, dims=(((1,), (0,)), ((), ()))):
    return lax.dot_general(a, b, dims, preferred_element_type=F32)


def gelu_pair(v):
    c = 0.7978845608028654
    sq = v * v
    t = jnp.tanh(c * (v + 0.044715 * (sq * v)))
    half = 0.5 * (1.0 + t)
    slope = half + 0.5 * v * (1.0 - t * t) * (c * (1.0 + 3.0 * 0.044715 * sq))
    return v * half, slope


def interleaver():
    r = lax.broadcasted_iota(jnp.int32, (2 * HALF, 2 * HALF), 0)
    c = lax.broadcasted_iota(jnp.int32, (2 * HALF, 2 * HALF), 1)
    p = (c >= HALF).astype(jnp.int32)
    return (r == 2 * (c - HALF * p) + p).astype(BF16)


def kernel(
    tok_hbm, keys_hbm, wi_hbm, wo_hbm, og_hbm,
    gt_hbm, gk_ref, gwi_hbm, gwo_hbm,
    tok_ref, keys_ref, wi, wo, og_ref, gt, gwi, gwo, wi_t, wo_t,
    dispatch, combine, mix,
    src1, dst1, rows, act, pre_grad, part, sib_in, chip_sum, par_in, src2, dst2,
    key_mine, key_sent, key_sib, key_split, key_got, key_row, key_rows, key_low, key_all,
    w_sem, o_sem, a1_s, a1_r, g_s, g_r, p_s, p_r, c_s, c_r, a2_s, a2_r,
    k_s, k_r,
):
    g = lax.axis_index("dp")
    e = lax.axis_index("expert")
    core, ylo = g % 2, g // 2
    x, y, z = e // (NY * NZ), (e // NZ) % NY, e % NZ
    sib = (g + 1 - 2 * core, e)
    par = ((g + 2) % 4, e)

    def nth(q, k):
        dy = ((k // 2) % 2) * 2 + (k // 16) % 2
        dx = ((k // 4) % 2) * 2 + (k // 32) % 2
        dz = 2 * ((k % 2) * 2 + (k // 8) % 2) + (q + dx + dy) % 2
        way = 1 - 2 * core
        xx, yy, zz = x + NX + way * dx, y + NY + way * dy, z + NZ + way * dz
        return (xx % NX) * (NY * NZ) + (yy % NY) * NZ + zz % NZ

    def near_by(k):
        low, zz = (ylo + k // NZ) % 2, (z + k) % NZ
        return low * NZ + zz, (low * 2 + core, x * (NY * NZ) + y * NZ + zz)

    def far_off(k):
        return (g, ((x + k // NY) % NX) * (NY * NZ) + ((y + k) % NY) * NZ + z)

    def copy(src, dst, s, r, dev):
        return pltpu.make_async_remote_copy(
            src_ref=src, dst_ref=dst, send_sem=s, recv_sem=r,
            device_id=dev, device_id_type=MESH,
        )

    loads = [
        pltpu.make_async_copy(far, near, w_sem.at[i])
        for i, (far, near) in enumerate((
            (tok_hbm, tok_ref), (keys_hbm, keys_ref), (og_hbm, og_ref), (wi_hbm, wi), (wo_hbm, wo)
        ))
    ]
    for load in loads:
        load.start()

    barrier = pltpu.get_barrier_semaphore()

    def greet(k, _):
        pl.semaphore_signal(barrier, inc=1, device_id=(g, (e + k) % NE), device_id_type=MESH)
        return 0

    lax.fori_loop(1, NE, greet, 0)
    pl.semaphore_signal(barrier, inc=1, device_id=sib, device_id_type=MESH)
    for k in range(NZ, 2 * NZ):
        pl.semaphore_signal(barrier, inc=1, device_id=near_by(k)[1], device_id_type=MESH)

    mix[...] = interleaver()

    def pairs(top, low):
        return dot(mix[...], jnp.concatenate([top, low], axis=0)).astype(BF16).reshape(HALF, 2, D)

    def apart(both):
        two = dot(mix[...], both.reshape(2 * HALF, D), TALL).astype(BF16)
        return two[:HALF], two[HALF:]

    loads[0].wait()
    loads[1].wait()
    tok = tok_ref[...]
    logits = dot(tok, keys_ref[...])
    ex = jnp.exp(logits - jnp.max(logits, axis=0, keepdims=True))
    disp = ex / jnp.sum(ex, axis=0, keepdims=True)
    ex = jnp.exp(logits - jnp.max(logits, axis=1, keepdims=True))
    comb = ex / jnp.sum(ex, axis=1, keepdims=True)
    dispatch[...] = disp
    combine[...] = comb
    slot_in = dot(disp.astype(BF16), tok, TALL).astype(BF16)
    loads[2].wait()
    slot_grad = dot(comb.astype(BF16), og_ref[...], TALL).astype(BF16)
    src1[0:HALF] = pairs(slot_in[:HALF], slot_grad[:HALF])
    src1[HALF:NE] = pairs(slot_in[HALF:], slot_grad[HALF:])
    own = e // 2
    dst1[0, pl.ds(own, 1)] = src1[pl.ds(e, 1)]

    loads[3].wait()
    loads[4].wait()
    wi_t[...] = wi[...].T
    wo_t[...] = wo[...].T
    pl.semaphore_wait(barrier, NE + NZ)

    def out_half(q):
        def step(k, _):
            t = nth(q, k)
            copy(src1.at[t], dst1.at[q, own], a1_s.at[q], a1_r.at[q], (g, t)).start()
            return 0

        lax.fori_loop(1 - q, HALF, step, 0)
        some = pl.ds(0, HALF - 1 + q)
        return copy(src1.at[some], dst1.at[q, some], a1_s.at[q], a1_r.at[q], sib)

    def back_half(q):
        def step(k, _):
            t = nth(q, k)
            copy(src2.at[q, t // 2], dst2.at[e], a2_s, a2_r, (g, t)).start()
            return 0

        lax.fori_loop(1 - q, HALF, step, 0)

    outs = [out_half(q) for q in range(2)]
    to_par = [copy(rows.at[:, q], rows.at[:, 4 + 2 * q], g_s.at[q], g_r.at[q], par) for q in range(2)]
    fwd = [
        copy(rows.at[:, 4 + 2 * q], rows.at[:, 5 + 2 * q], g_s.at[2 + q], g_r.at[2 + q], sib)
        for q in range(2)
    ]
    to_sib = copy(rows.at[:, pl.ds(0, 2)], rows.at[:, pl.ds(2, 2)], g_s.at[4], g_r.at[4], sib)
    for q in range(2):
        outs[q].wait_recv()
        rows[0, q], rows[1, q] = apart(dst1[q])
        to_par[q].start()
    to_sib.start()

    def expert(i):
        at = pl.ds(2 * i, 2)
        value, slope = gelu_pair(dot(rows[0, at].reshape(NE, D), wi[...]))
        value = value.astype(BF16)
        act[i] = value
        down = (dot(rows[1, at].reshape(NE, D), wo_t[...]) * slope).astype(BF16)
        pre_grad[i] = down
        part[0, at] = dot(value, wo[...]).astype(BF16).reshape(2, HALF, D)
        part[1, at] = dot(down, wi_t[...]).astype(BF16).reshape(2, HALF, D)

    give = [
        copy(part.at[:, 5 + 2 * q], sib_in.at[:, 2 + q], p_s.at[q], p_r.at[q], sib) for q in range(2)
    ]
    give_near = copy(part.at[:, pl.ds(2, 2)], sib_in.at[:, pl.ds(0, 2)], p_s.at[2], p_r.at[2], sib)
    cross = [copy(chip_sum.at[:, q], par_in.at[:, q], c_s.at[q], c_r.at[q], par) for q in range(2)]

    def add_up(q):
        give[q].wait_recv()
        chip_sum[:, q] = (part[:, 4 + 2 * q].astype(F32) + sib_in[:, 2 + q].astype(F32)).astype(BF16)
        cross[q].start()

    expert(0)
    to_par[0].wait_recv()
    fwd[0].start()
    to_sib.wait_recv()
    expert(1)
    give_near.start()
    fwd[0].wait_recv()
    expert(2)
    give[0].start()
    to_par[1].wait_recv()
    fwd[1].start()
    add_up(0)
    fwd[1].wait_recv()
    expert(3)
    give[1].start()
    add_up(1)

    store_o = pltpu.make_async_copy(gwo, gwo_hbm, o_sem.at[0])
    store_i = pltpu.make_async_copy(gwi, gwi_hbm, o_sem.at[1])
    store_t = pltpu.make_async_copy(gt, gt_hbm, o_sem.at[2])
    give_near.wait_recv()
    for q in range(2):
        near = part[:, q].astype(F32) + sib_in[:, q].astype(F32)
        cross[q].wait_recv()
        total = (near + par_in[:, q].astype(F32)).astype(BF16)
        src2[q] = pairs(total[0], total[1])
        if q == 0:
            dst2[pl.ds(e, 1)] = src2[0, pl.ds(own, 1)]
        back_half(q)
    backs = copy(dst2.at[pl.ds(0, NE - 1)], dst2.at[pl.ds(0, NE - 1)], a2_s, a2_r, sib)

    gwo[...] = dot(act[...].reshape(4 * NE, D), rows[1].reshape(4 * NE, D), TALL).astype(BF16)
    store_o.start()
    gwi[...] = dot(rows[0].reshape(4 * NE, D), pre_grad[...].reshape(4 * NE, D), TALL).astype(BF16)
    store_i.start()
    backs.wait_recv()

    low, high = apart(dst2[0:HALF]), apart(dst2[HALF:NE])
    slot_out = jnp.concatenate([low[0], high[0]], axis=0)
    slot_in_grad = jnp.concatenate([low[1], high[1]], axis=0)
    tok = tok_ref[...]
    cg = dot(og_ref[...], slot_out, WIDE)
    dg = dot(tok, slot_in_grad, WIDE)
    comb = combine[...]
    disp = dispatch[...]
    lg = comb * (cg - jnp.sum(comb * cg, axis=1, keepdims=True))
    lg = lg + disp * (dg - jnp.sum(disp * dg, axis=0, keepdims=True))
    lg = lg.astype(BF16)
    term = dot(lg, tok, TALL)

    key_mine[...] = term.reshape(2, HALF, D)
    key_sent[...] = key_mine[1 - core].astype(BF16)
    k0 = copy(key_sent, key_sib, k_s.at[0], k_r.at[0], sib)
    k0.start()
    grad = dot(disp.astype(BF16), slot_in_grad) + dot(lg, keys_ref[...], WIDE)
    gt[...] = grad.astype(BF16)
    store_t.start()
    k0.wait_recv()
    key_split[...] = (key_mine[core] + key_sib[...].astype(F32)).astype(BF16).reshape(16, 4, D)
    mine = ylo * NZ + z

    def scatter(k, _):
        t, dev = near_by(k)
        copy(key_split.at[t], key_got.at[mine], k_s.at[1], k_r.at[1], dev).start()
        return 0

    lax.fori_loop(1, 16, scatter, 0)
    key_got[pl.ds(mine, 1)] = key_split[pl.ds(mine, 1)]
    k1 = copy(key_split.at[pl.ds(0, 15)], key_got.at[pl.ds(0, 15)], k_s.at[1], k_r.at[1], sib)
    k1.wait_recv()
    row = jnp.sum(key_got[...].astype(F32), axis=0).astype(BF16)
    place = x * NY + y
    key_row[...] = row[None]
    key_rows[pl.ds(place, 1)] = row[None]

    def share(k, _):
        copy(key_row.at[0], key_rows.at[place], k_s.at[2], k_r.at[2], far_off(k)).start()
        return 0

    lax.fori_loop(1, 16, share, 0)
    k2 = copy(key_rows.at[pl.ds(0, 15)], key_rows.at[pl.ds(0, 15)], k_s.at[2], k_r.at[2], sib)
    k2.wait_recv()
    row = jnp.sum(key_rows[...].astype(F32), axis=0).astype(BF16)
    key_low[...] = row[None]
    key_all[pl.ds(core * 16 + mine, 1)] = row[None]

    def spread(k, _):
        copy(key_low.at[0], key_all.at[core * 16 + mine], k_s.at[3], k_r.at[3], near_by(k)[1]).start()
        return 0

    lax.fori_loop(1, 16, spread, 0)
    k3 = copy(key_split.at[pl.ds(0, 15)], key_got.at[pl.ds(0, 15)], k_s.at[3], k_r.at[3], sib)
    k3.wait_recv()
    held = key_all.at[pl.ds(core * 16, 16)]
    k4 = copy(held, held, k_s.at[4], k_r.at[4], sib)
    k4.start()
    k4.wait_recv()
    gk_ref[...] = key_all[...].reshape(NE, D)

    for store in (store_o, store_i, store_t):
        store.wait()
    for done in outs + to_par + fwd + [to_sib] + give + [give_near] + cross + [backs, k0, k1, k2, k3, k4]:
        done.wait_send()


def hand_over(gt, gk, gwi, gwo, gt_out, gk_out, gwi_out, gwo_out, t, k, turned, i, o, load_sem, store_sem):
    def move(n, a, b):
        return pltpu.make_async_copy(a, b, n)

    loads = [
        move(load_sem.at[n], a, b) for n, (a, b) in enumerate(((gk, k), (gt, t), (gwi, i), (gwo, o)))
    ]
    stores = [
        move(store_sem.at[n], a, b)
        for n, (a, b) in enumerate(((turned, gk_out), (t, gt_out), (i, gwi_out), (o, gwo_out)))
    ]
    for load in loads:
        load.start()
    loads[0].wait()
    turned[...] = k[...].astype(F32).T
    stores[0].start()
    for n in range(1, 4):
        loads[n].wait()
        stores[n].start()
    for store in stores:
        store.wait()


def body(tokens, slot_keys, w_input, w_output, output_grad):
    vm = pl.BlockSpec(memory_space=pltpu.VMEM)
    anywhere = pl.BlockSpec(memory_space=pl.ANY)
    dma = pltpu.SemaphoreType.DMA
    n = NE
    gt, gk, gwi, gwo = pl.pallas_call(
        kernel,
        out_shape=(
            jax.ShapeDtypeStruct((256, D), BF16),
            jax.ShapeDtypeStruct((n, D), BF16),
            jax.ShapeDtypeStruct((D, D), BF16),
            jax.ShapeDtypeStruct((D, D), BF16),
        ),
        in_specs=[anywhere] * 5,
        out_specs=[anywhere, vm, anywhere, anywhere],
        scratch_shapes=[
            pltpu.VMEM((256, D), BF16),
            pltpu.VMEM((D, n), BF16),
            pltpu.VMEM((D, D), BF16),
            pltpu.VMEM((D, D), BF16),
            pltpu.VMEM((256, D), BF16),
            pltpu.VMEM((256, D), BF16),
            pltpu.VMEM((D, D), BF16),
            pltpu.VMEM((D, D), BF16),
            pltpu.VMEM((D, D), BF16),
            pltpu.VMEM((D, D), BF16),
            pltpu.VMEM((256, n), F32),
            pltpu.VMEM((256, n), F32),
            pltpu.VMEM((n, n), BF16),
            pltpu.VMEM((n, 2, D), BF16),
            pltpu.VMEM((2, HALF, 2, D), BF16),
            pltpu.VMEM((2, 8, HALF, D), BF16),
            pltpu.VMEM((4, n, D), BF16),
            pltpu.VMEM((4, n, D), BF16),
            pltpu.VMEM((2, 8, HALF, D), BF16),
            pltpu.VMEM((2, 4, HALF, D), BF16),
            pltpu.VMEM((2, 2, HALF, D), BF16),
            pltpu.VMEM((2, 2, HALF, D), BF16),
            pltpu.VMEM((2, HALF, 2, D), BF16),
            pltpu.VMEM((n, 2, D), BF16),
            pltpu.VMEM((2, HALF, D), F32),
            pltpu.VMEM((HALF, D), BF16),
            pltpu.VMEM((HALF, D), BF16),
            pltpu.VMEM((16, 4, D), BF16),
            pltpu.VMEM((16, 4, D), BF16),
            pltpu.VMEM((1, 4, D), BF16),
            pltpu.VMEM((16, 4, D), BF16),
            pltpu.VMEM((1, 4, D), BF16),
            pltpu.VMEM((32, 4, D), BF16),
            dma((5,)), dma((3,)), dma((2,)), dma((2,)), dma((5,)), dma((5,)), dma((3,)), dma((3,)),
            dma((2,)), dma((2,)), dma, dma,
            dma((5,)), dma((5,)),
        ],
        compiler_params=pltpu.CompilerParams(
            collective_id=0, has_side_effects=True, vmem_limit_bytes=60 << 20
        ),
    )(tokens[0], slot_keys, w_input[0], w_output[0], output_grad[0])
    gt, gk, gwi, gwo = pl.pallas_call(
        hand_over,
        out_shape=(
            jax.ShapeDtypeStruct((256, D), BF16),
            jax.ShapeDtypeStruct((D, n), F32),
            jax.ShapeDtypeStruct((D, D), BF16),
            jax.ShapeDtypeStruct((D, D), BF16),
        ),
        in_specs=[anywhere] * 4,
        out_specs=[anywhere] * 4,
        scratch_shapes=[
            pltpu.VMEM((256, D), BF16),
            pltpu.VMEM((n, D), BF16),
            pltpu.VMEM((D, n), F32),
            pltpu.VMEM((D, D), BF16),
            pltpu.VMEM((D, D), BF16),
            dma((4,)),
            dma((4,)),
        ],
        compiler_params=pltpu.CompilerParams(vmem_limit_bytes=60 << 20),
    )(gt, gk, gwi, gwo)
    return gt[None], gk, gwi[None], gwo[None]


def solution(mesh):
    placed = (
        P(("dp", "expert"), None, None),
        P(),
        P("expert", None, "dp"),
        P("expert", "dp", None),
        P(("dp", "expert"), None, None),
    )
    return jax.shard_map(
        body,
        mesh=mesh,
        in_specs=placed,
        out_specs=(
            P(("dp", "expert"), None, None),
            P(),
            P("expert", None, "dp"),
            P("expert", "dp", None),
        ),
        check_vma=False,
    )
```

```python
import functools

import jax
import jax.numpy as jnp
from jax import lax
from jax.experimental import pallas as pl
from jax.experimental.pallas import tpu as pltpu
from jax.sharding import PartitionSpec as P

MESH = pl.DeviceIdType.MESH
F32 = jnp.float32
BF16 = jnp.bfloat16
NX, NY, NZ = 4, 4, 8
NE = NX * NY * NZ
HALF = NE // 2
D = 640
TALL = (((0,), (0,)), ((), ()))
WIDE = (((1,), (1,)), ((), ()))


def dot(a, b, dims=(((1,), (0,)), ((), ()))):
    return lax.dot_general(a, b, dims, preferred_element_type=F32)


def gelu_pair(v):
    c = 0.7978845608028654
    sq = v * v
    t = jnp.tanh(c * (v + 0.044715 * (sq * v)))
    half = 0.5 * (1.0 + t)
    slope = half + 0.5 * v * (1.0 - t * t) * (c * (1.0 + 3.0 * 0.044715 * sq))
    return v * half, slope


def interleaver():
    r = lax.broadcasted_iota(jnp.int32, (2 * HALF, 2 * HALF), 0)
    c = lax.broadcasted_iota(jnp.int32, (2 * HALF, 2 * HALF), 1)
    p = (c >= HALF).astype(jnp.int32)
    return (r == 2 * (c - HALF * p) + p).astype(BF16)


def kernel(
    tok_hbm, keys_hbm, wi_hbm, wo_hbm, og_hbm,
    gt_hbm, gk_ref, gwi_hbm, gwo_hbm,
    tok_ref, keys_ref, wi, wo, og_ref, gt, gwi, gwo, wi_t, wo_t,
    dispatch, combine, mix,
    src1, dst1, rows, act, pre_grad, part, sib_in, chip_sum, par_in, src2, dst2,
    key_mine, key_sib, key_split, key_got, key_row, key_rows, key_low, key_all,
    w_sem, o_sem, a1_s, a1_r, g_s, g_r, p_s, p_r, c_s, c_r, a2_s, a2_r,
    k_s, k_r,
):
    g = lax.axis_index("dp")
    e = lax.axis_index("expert")
    core, ylo = g % 2, g // 2
    x, y, z = e // (NY * NZ), (e // NZ) % NY, e % NZ
    sib = (g + 1 - 2 * core, e)
    par = ((g + 2) % 4, e)

    def nth(q, k):
        k = HALF - q - k
        dy = ((k // 2) % 2) * 2 + (k // 16) % 2
        dx = ((k // 4) % 2) * 2 + (k // 32) % 2
        dz = 2 * ((k % 2) * 2 + (k // 8) % 2) + (q + dx + dy) % 2
        return ((x + dx) % NX) * (NY * NZ) + ((y + dy) % NY) * NZ + (z + dz) % NZ

    def near_by(k):
        low, zz = (ylo + k // NZ) % 2, (z + k) % NZ
        return low * NZ + zz, (low * 2 + core, x * (NY * NZ) + y * NZ + zz)

    def far_off(k):
        return (g, ((x + k // NY) % NX) * (NY * NZ) + ((y + k) % NY) * NZ + z)

    def copy(src, dst, s, r, dev):
        return pltpu.make_async_remote_copy(
            src_ref=src, dst_ref=dst, send_sem=s, recv_sem=r,
            device_id=dev, device_id_type=MESH,
        )

    loads = [
        pltpu.make_async_copy(far, near, w_sem.at[i])
        for i, (far, near) in enumerate((
            (tok_hbm, tok_ref), (keys_hbm, keys_ref), (og_hbm, og_ref), (wi_hbm, wi), (wo_hbm, wo)
        ))
    ]
    for load in loads:
        load.start()

    barrier = pltpu.get_barrier_semaphore()

    def greet(k, _):
        pl.semaphore_signal(barrier, inc=1, device_id=(g, (e + k) % NE), device_id_type=MESH)
        return 0

    lax.fori_loop(1, NE, greet, 0)
    pl.semaphore_signal(barrier, inc=1, device_id=sib, device_id_type=MESH)
    for k in range(NZ, 2 * NZ):
        pl.semaphore_signal(barrier, inc=1, device_id=near_by(k)[1], device_id_type=MESH)

    mix[...] = interleaver()

    def pairs(top, low):
        return dot(mix[...], jnp.concatenate([top, low], axis=0)).astype(BF16).reshape(HALF, 2, D)

    def apart(both):
        two = dot(mix[...], both.reshape(2 * HALF, D), TALL).astype(BF16)
        return two[:HALF], two[HALF:]

    loads[0].wait()
    loads[1].wait()
    tok = tok_ref[...]
    logits = dot(tok, keys_ref[...])
    ex = jnp.exp(logits - jnp.max(logits, axis=0, keepdims=True))
    disp = ex / jnp.sum(ex, axis=0, keepdims=True)
    ex = jnp.exp(logits - jnp.max(logits, axis=1, keepdims=True))
    comb = ex / jnp.sum(ex, axis=1, keepdims=True)
    dispatch[...] = disp
    combine[...] = comb
    slot_in = dot(disp.astype(BF16), tok, TALL).astype(BF16)
    loads[2].wait()
    slot_grad = dot(comb.astype(BF16), og_ref[...], TALL).astype(BF16)
    src1[0:HALF] = pairs(slot_in[:HALF], slot_grad[:HALF])
    src1[HALF:NE] = pairs(slot_in[HALF:], slot_grad[HALF:])
    own = e // 2
    dst1[0, pl.ds(own, 1)] = src1[pl.ds(e, 1)]

    loads[3].wait()
    loads[4].wait()
    wi_t[...] = wi[...].T
    wo_t[...] = wo[...].T
    pl.semaphore_wait(barrier, NE + NZ)

    def out_half(q):
        def step(k, _):
            t = nth(q, k)
            copy(src1.at[t], dst1.at[q, own], a1_s.at[q], a1_r.at[q], (g, t)).start()
            return 0

        lax.fori_loop(1 - q, HALF, step, 0)
        some = pl.ds(0, HALF - 1 + q)
        return copy(src1.at[some], dst1.at[q, some], a1_s.at[q], a1_r.at[q], sib)

    def back_half(q):
        def step(k, _):
            t = nth(q, k)
            copy(src2.at[q, t // 2], dst2.at[e], a2_s, a2_r, (g, t)).start()
            return 0

        lax.fori_loop(1 - q, HALF, step, 0)

    outs = [out_half(q) for q in range(2)]
    to_par = [copy(rows.at[:, q], rows.at[:, 4 + 2 * q], g_s.at[q], g_r.at[q], par) for q in range(2)]
    fwd = [
        copy(rows.at[:, 4 + 2 * q], rows.at[:, 5 + 2 * q], g_s.at[2 + q], g_r.at[2 + q], sib)
        for q in range(2)
    ]
    to_sib = copy(rows.at[:, pl.ds(0, 2)], rows.at[:, pl.ds(2, 2)], g_s.at[4], g_r.at[4], sib)
    for q in range(2):
        outs[q].wait_recv()
        rows[0, q], rows[1, q] = apart(dst1[q])
        to_par[q].start()
    to_sib.start()

    def expert(i):
        at = pl.ds(2 * i, 2)
        value, slope = gelu_pair(dot(rows[0, at].reshape(NE, D), wi[...]))
        value = value.astype(BF16)
        act[i] = value
        down = (dot(rows[1, at].reshape(NE, D), wo_t[...]) * slope).astype(BF16)
        pre_grad[i] = down
        part[0, at] = dot(value, wo[...]).astype(BF16).reshape(2, HALF, D)
        part[1, at] = dot(down, wi_t[...]).astype(BF16).reshape(2, HALF, D)

    give = [
        copy(part.at[:, 5 + 2 * q], sib_in.at[:, 2 + q], p_s.at[q], p_r.at[q], sib) for q in range(2)
    ]
    give_near = copy(part.at[:, pl.ds(2, 2)], sib_in.at[:, pl.ds(0, 2)], p_s.at[2], p_r.at[2], sib)
    cross = [copy(chip_sum.at[:, q], par_in.at[:, q], c_s.at[q], c_r.at[q], par) for q in range(2)]

    def add_up(q):
        give[q].wait_recv()
        chip_sum[:, q] = (part[:, 4 + 2 * q].astype(F32) + sib_in[:, 2 + q].astype(F32)).astype(BF16)
        cross[q].start()

    expert(0)
    to_par[0].wait_recv()
    fwd[0].start()
    to_sib.wait_recv()
    expert(1)
    give_near.start()
    fwd[0].wait_recv()
    expert(2)
    give[0].start()
    to_par[1].wait_recv()
    fwd[1].start()
    add_up(0)
    fwd[1].wait_recv()
    expert(3)
    give[1].start()
    add_up(1)

    store_o = pltpu.make_async_copy(gwo, gwo_hbm, o_sem.at[0])
    store_i = pltpu.make_async_copy(gwi, gwi_hbm, o_sem.at[1])
    store_t = pltpu.make_async_copy(gt, gt_hbm, o_sem.at[2])
    give_near.wait_recv()
    for q in range(2):
        near = part[:, q].astype(F32) + sib_in[:, q].astype(F32)
        cross[q].wait_recv()
        total = (near + par_in[:, q].astype(F32)).astype(BF16)
        src2[q] = pairs(total[0], total[1])
        if q == 0:
            dst2[pl.ds(e, 1)] = src2[0, pl.ds(own, 1)]
        back_half(q)
    backs = copy(dst2.at[pl.ds(0, NE - 1)], dst2.at[pl.ds(0, NE - 1)], a2_s, a2_r, sib)

    gwo[...] = dot(act[...].reshape(4 * NE, D), rows[1].reshape(4 * NE, D), TALL).astype(BF16)
    store_o.start()
    gwi[...] = dot(rows[0].reshape(4 * NE, D), pre_grad[...].reshape(4 * NE, D), TALL).astype(BF16)
    store_i.start()
    backs.wait_recv()

    low, high = apart(dst2[0:HALF]), apart(dst2[HALF:NE])
    slot_out = jnp.concatenate([low[0], high[0]], axis=0)
    slot_in_grad = jnp.concatenate([low[1], high[1]], axis=0)
    tok = tok_ref[...]
    cg = dot(og_ref[...], slot_out, WIDE)
    dg = dot(tok, slot_in_grad, WIDE)
    comb = combine[...]
    disp = dispatch[...]
    lg = comb * (cg - jnp.sum(comb * cg, axis=1, keepdims=True))
    lg = lg + disp * (dg - jnp.sum(disp * dg, axis=0, keepdims=True))
    lg = lg.astype(BF16)
    term = dot(lg, tok, TALL)

    key_mine[...] = term.reshape(2, HALF, D)
    k0 = copy(key_mine.at[1 - core], key_sib, k_s.at[0], k_r.at[0], sib)
    k0.start()
    grad = dot(disp.astype(BF16), slot_in_grad) + dot(lg, keys_ref[...], WIDE)
    gt[...] = grad.astype(BF16)
    store_t.start()
    k0.wait_recv()
    key_split[...] = (key_mine[core] + key_sib[...]).astype(BF16).reshape(16, 4, D)
    mine = ylo * NZ + z

    def scatter(k, _):
        t, dev = near_by(k)
        copy(key_split.at[t], key_got.at[mine], k_s.at[1], k_r.at[1], dev).start()
        return 0

    lax.fori_loop(1, 16, scatter, 0)
    key_got[pl.ds(mine, 1)] = key_split[pl.ds(mine, 1)]
    k1 = copy(key_split.at[pl.ds(0, 15)], key_got.at[pl.ds(0, 15)], k_s.at[1], k_r.at[1], sib)
    k1.wait_recv()
    row = jnp.sum(key_got[...].astype(F32), axis=0).astype(BF16)
    place = x * NY + y
    key_row[...] = row[None]
    key_rows[pl.ds(place, 1)] = row[None]

    def share(k, _):
        copy(key_row.at[0], key_rows.at[place], k_s.at[2], k_r.at[2], far_off(k)).start()
        return 0

    lax.fori_loop(1, 16, share, 0)
    k2 = copy(key_rows.at[pl.ds(0, 15)], key_rows.at[pl.ds(0, 15)], k_s.at[2], k_r.at[2], sib)
    k2.wait_recv()
    row = jnp.sum(key_rows[...].astype(F32), axis=0).astype(BF16)
    key_low[...] = row[None]
    key_all[pl.ds(core * 16 + mine, 1)] = row[None]

    def spread(k, _):
        copy(key_low.at[0], key_all.at[core * 16 + mine], k_s.at[3], k_r.at[3], near_by(k)[1]).start()
        return 0

    lax.fori_loop(1, 16, spread, 0)
    k3 = copy(key_split.at[pl.ds(0, 15)], key_got.at[pl.ds(0, 15)], k_s.at[3], k_r.at[3], sib)
    k3.wait_recv()
    held = key_all.at[pl.ds(core * 16, 16)]
    k4 = copy(held, held, k_s.at[4], k_r.at[4], sib)
    k4.start()
    k4.wait_recv()
    gk_ref[...] = key_all[...].reshape(NE, D)

    for store in (store_o, store_i, store_t):
        store.wait()
    for done in outs + to_par + fwd + [to_sib] + give + [give_near] + cross + [backs, k0, k1, k2, k3, k4]:
        done.wait_send()


def hand_over(gt, gk, gwi, gwo, gt_out, gk_out, gwi_out, gwo_out, t, k, turned, i, o, load_sem, store_sem):
    def move(n, a, b):
        return pltpu.make_async_copy(a, b, n)

    loads = [
        move(load_sem.at[n], a, b) for n, (a, b) in enumerate(((gk, k), (gt, t), (gwi, i), (gwo, o)))
    ]
    stores = [
        move(store_sem.at[n], a, b)
        for n, (a, b) in enumerate(((turned, gk_out), (t, gt_out), (i, gwi_out), (o, gwo_out)))
    ]
    for load in loads:
        load.start()
    loads[0].wait()
    turned[...] = k[...].astype(F32).T
    stores[0].start()
    for n in range(1, 4):
        loads[n].wait()
        stores[n].start()
    for store in stores:
        store.wait()


def body(tokens, slot_keys, w_input, w_output, output_grad):
    vm = pl.BlockSpec(memory_space=pltpu.VMEM)
    anywhere = pl.BlockSpec(memory_space=pl.ANY)
    dma = pltpu.SemaphoreType.DMA
    n = NE
    gt, gk, gwi, gwo = pl.pallas_call(
        kernel,
        out_shape=(
            jax.ShapeDtypeStruct((256, D), BF16),
            jax.ShapeDtypeStruct((n, D), BF16),
            jax.ShapeDtypeStruct((D, D), BF16),
            jax.ShapeDtypeStruct((D, D), BF16),
        ),
        in_specs=[anywhere] * 5,
        out_specs=[anywhere, vm, anywhere, anywhere],
        scratch_shapes=[
            pltpu.VMEM((256, D), BF16),
            pltpu.VMEM((D, n), BF16),
            pltpu.VMEM((D, D), BF16),
            pltpu.VMEM((D, D), BF16),
            pltpu.VMEM((256, D), BF16),
            pltpu.VMEM((256, D), BF16),
            pltpu.VMEM((D, D), BF16),
            pltpu.VMEM((D, D), BF16),
            pltpu.VMEM((D, D), BF16),
            pltpu.VMEM((D, D), BF16),
            pltpu.VMEM((256, n), F32),
            pltpu.VMEM((256, n), F32),
            pltpu.VMEM((n, n), BF16),
            pltpu.VMEM((n, 2, D), BF16),
            pltpu.VMEM((2, HALF, 2, D), BF16),
            pltpu.VMEM((2, 8, HALF, D), BF16),
            pltpu.VMEM((4, n, D), BF16),
            pltpu.VMEM((4, n, D), BF16),
            pltpu.VMEM((2, 8, HALF, D), BF16),
            pltpu.VMEM((2, 4, HALF, D), BF16),
            pltpu.VMEM((2, 2, HALF, D), BF16),
            pltpu.VMEM((2, 2, HALF, D), BF16),
            pltpu.VMEM((2, HALF, 2, D), BF16),
            pltpu.VMEM((n, 2, D), BF16),
            pltpu.VMEM((2, HALF, D), F32),
            pltpu.VMEM((HALF, D), F32),
            pltpu.VMEM((16, 4, D), BF16),
            pltpu.VMEM((16, 4, D), BF16),
            pltpu.VMEM((1, 4, D), BF16),
            pltpu.VMEM((16, 4, D), BF16),
            pltpu.VMEM((1, 4, D), BF16),
            pltpu.VMEM((32, 4, D), BF16),
            dma((5,)), dma((3,)), dma((2,)), dma((2,)), dma((5,)), dma((5,)), dma((3,)), dma((3,)),
            dma((2,)), dma((2,)), dma, dma,
            dma((5,)), dma((5,)),
        ],
        compiler_params=pltpu.CompilerParams(
            collective_id=0, has_side_effects=True, vmem_limit_bytes=60 << 20
        ),
    )(tokens[0], slot_keys, w_input[0], w_output[0], output_grad[0])
    gt, gk, gwi, gwo = pl.pallas_call(
        hand_over,
        out_shape=(
            jax.ShapeDtypeStruct((256, D), BF16),
            jax.ShapeDtypeStruct((D, n), F32),
            jax.ShapeDtypeStruct((D, D), BF16),
            jax.ShapeDtypeStruct((D, D), BF16),
        ),
        in_specs=[anywhere] * 4,
        out_specs=[anywhere] * 4,
        scratch_shapes=[
            pltpu.VMEM((256, D), BF16),
            pltpu.VMEM((n, D), BF16),
            pltpu.VMEM((D, n), F32),
            pltpu.VMEM((D, D), BF16),
            pltpu.VMEM((D, D), BF16),
            dma((4,)),
            dma((4,)),
        ],
        compiler_params=pltpu.CompilerParams(vmem_limit_bytes=60 << 20),
    )(gt, gk, gwi, gwo)
    return gt[None], gk, gwi[None], gwo[None]


def solution(mesh):
    placed = (
        P(("dp", "expert"), None, None),
        P(),
        P("expert", None, "dp"),
        P("expert", "dp", None),
        P(("dp", "expert"), None, None),
    )
    return jax.shard_map(
        body,
        mesh=mesh,
        in_specs=placed,
        out_specs=(
            P(("dp", "expert"), None, None),
            P(),
            P("expert", None, "dp"),
            P("expert", "dp", None),
        ),
        check_vma=False,
    )
```
